32 devices in a mesh: gx: 8 (over z, x), gy: 4 (over y, core).
Axes of the slice: x: 2, y: 2, z: 4, core: 2. Of those that a mesh axis runs over, the one named last changes fastest.
Arguments:
- velocity: float32 [3, 128, 128, 128], P(None, 'gx', 'gy'), may hold values from -3 to 3
- theta: float32 [128, 128, 128], P('gx', 'gy'), may hold values from -4 to 4
- vapour: float32 [128, 128, 128], P('gx', 'gy'), may hold values from 0.5 to 1.5
- radius_sq: float32 [64, 1024], P(None, ('gx', 'gy')), may hold values from 0.5 to 2
- multiplicity: float32 [64, 1024], P(None, ('gx', 'gy')), may hold values from 0.5 to 2
- counts: int32 [1024], P(('gx', 'gy')), may hold values from 16 to 64
- pairing: int32 [1024, 64], P(('gx', 'gy')), may hold values from 0 to 63, each once within a row
- destination: int32 [64, 1024], P(None, ('gx', 'gy')), may hold values from 0 to 1023, as said below
Outputs:
- velocity_new: float32 [3, 128, 128, 128], P(None, 'gx', 'gy')
- theta_new: float32 [128, 128, 128], P('gx', 'gy')
- vapour_new: float32 [128, 128, 128], P('gx', 'gy')
- moments: float32 [3, 1024], P(None, ('gx', 'gy'))
The draws below stay inside these ranges and needn't reach their ends.
Inputs may be any that keep to these rules, and one draw needn't show every extreme that they name: Each slot's destination is its own box or one of the eight boxes around it, with box columns wrapping around 32 and box rows around 32, numbered as in the reference program. `pairing`: each row is a permutation of 0 to 63.
All inputs are finite; a program needn't handle non-finite values.
Results may differ from the reference program's by a relative error of at most 0.0003.
Values sent between devices are 32-bit elements; how exact they have to be, the bound alone decides.
No kernel may reach another device: no remote copies, remote signals or barrier semaphores. Data moves between devices by JAX's collectives and lax.ppermute only.
A program may use at most 64 MiB of HBM per device.

```python
import math
import jax
import jax.numpy as jnp
from jax import lax

NZ = 128
BW = 4
SLOTS = 64
NX = 128
NY = 128
BXD = 4
BYD = 8
BOX_DEV = 32
BOXES = 1024
NBX = 32
NBY = 32
N_GX = 8
N_GY = 4


def draw_destination(key, part):
    own_key = jax.random.fold_in(key, 11)
    key_x, key_y = jax.random.split(own_key)
    step_x = jax.random.randint(key_x, (SLOTS, BOXES), -1, 2)
    step_y = jax.random.randint(key_y, (SLOTS, BOXES), -1, 2)
    box_number = jnp.arange(BOXES)
    device_number = box_number // BOX_DEV
    local_number = box_number % BOX_DEV
    grid_rows = NBY // BYD
    column = device_number // grid_rows * BXD + local_number // BYD
    row_index = device_number % grid_rows * BYD + local_number % BYD
    target_x = (column[None, :] + step_x) % NBX
    target_y = (row_index[None, :] + step_y) % NBY
    target = (target_x // BXD * grid_rows + target_y // BYD) * BOX_DEV + target_x % BXD * BYD + target_y % BYD
    return target.astype(jnp.int32)


def place_ends(result, stream_key, smallest, top_value):
    place = [jax.random.randint(jax.random.fold_in(stream_key, axis), (), 0, length) for axis, length in enumerate(result.shape)]
    widest = result.shape.index(max(result.shape))
    neighbour = place[:widest] + [(place[widest] + 1) % result.shape[widest]] + place[widest + 1:]
    return result.at[tuple(place)].set(smallest).at[tuple(neighbour)].set(top_value)


def shard_levels(stream_key, shape, shards, low, top_value):
    def one(axis_at, parts):
        heights = jax.random.uniform(jax.random.fold_in(jax.random.fold_in(stream_key, 6), axis_at), (parts,), jnp.float32, low / len(shards), top_value / len(shards))
        return jnp.repeat(jnp.exp(heights), shape[axis_at] // parts).reshape((-1,) + (1,) * (len(shape) - axis_at - 1))

    factor_of = one(*shards[0])
    for cut in shards[1:]:
        factor_of = factor_of * one(*cut)
    return factor_of


def normal_values(key, extent, deviation, most, pieces=(), dtype=jnp.bfloat16):
    gain = shard_levels(key, extent, pieces, -0.22, 0.18) if pieces else 1.0
    drawn = jax.random.normal(key, extent, jnp.float32) * deviation * gain
    return jnp.minimum(jnp.maximum(drawn, -most), most).astype(dtype)


def setup_inputs(seed: int = 0) -> dict:
    arg_keys = jax.random.split(jax.random.key(seed), 9)
    velocity = normal_values(arg_keys[0], (3, NX, NY, NZ), 0.5, 3.0, ((1, 8), (2, 4)), jnp.float32)
    theta = normal_values(arg_keys[1], (NX, NY, NZ), 1.0, 4.0, ((0, 8), (1, 4)), jnp.float32)
    vapour = jnp.clip(0.5 + 1.0 * jax.random.uniform(arg_keys[2], (NX, NY, NZ), jnp.float32) ** shard_levels(arg_keys[2], (NX, NY, NZ), ((0, 8), (1, 4)), -0.2, 0.2), 0.5, 1.5)
    radius_sq = jnp.clip(jnp.exp(math.log(2.0) - 1.3862944 * jax.random.uniform(arg_keys[3], (SLOTS, BOXES), jnp.float32) ** shard_levels(arg_keys[3], (SLOTS, BOXES), ((1, 32),), -0.2, 0.2)), 0.5, 2.0)
    multiplicity = jnp.clip(jnp.exp(math.log(2.0) - 1.3862944 * jax.random.uniform(arg_keys[4], (SLOTS, BOXES), jnp.float32) ** shard_levels(arg_keys[4], (SLOTS, BOXES), ((1, 32),), -0.2, 0.2)), 0.5, 2.0)
    counts = place_ends(jax.random.randint(arg_keys[5], (BOXES,), SLOTS // 4, SLOTS + 1), jax.random.fold_in(arg_keys[5], 1), SLOTS // 4, SLOTS).astype(jnp.int32)
    pairing = jax.vmap(lambda own: jax.random.permutation(own, SLOTS))(jax.random.split(arg_keys[6], BOXES)).reshape((BOXES, SLOTS)).astype(jnp.int32)
    destination = draw_destination(jax.random.fold_in(arg_keys[8], 71), 0)
    return dict(velocity=velocity, theta=theta, vapour=vapour, radius_sq=radius_sq, multiplicity=multiplicity, counts=counts, pairing=pairing, destination=destination)


TIME_STEP = 0.2
DIFFUSION = 0.05
BUOYANCY = 0.5
GROWTH = 0.5
COLLISION = 0.05
CONDENSE = 0.002
HIGHEST = lax.Precision.HIGHEST

def vertical_pair(values):
    upper_cell = jnp.concatenate([values[..., 1:], values[..., -1:]], axis=-1)
    lower_cell = jnp.concatenate([values[..., :1], values[..., :-1]], axis=-1)
    return (upper_cell, lower_cell)

def advect_one(values, speed_x, speed_y, speed_z):
    east_cell = jnp.roll(values, -1, 0)
    west_cell = jnp.roll(values, 1, 0)
    north_cell = jnp.roll(values, -1, 1)
    south_cell = jnp.roll(values, 1, 1)
    upper_cell, lower_cell = vertical_pair(values)
    carried = -0.5 * (speed_x * (east_cell - west_cell) + speed_y * (north_cell - south_cell) + speed_z * (upper_cell - lower_cell))
    spread = east_cell + west_cell + north_cell + south_cell + upper_cell + lower_cell - 6.0 * values
    return values + TIME_STEP * (carried + DIFFUSION * spread)

def cosine_table(levels):
    level_index = jnp.arange(levels).astype(jnp.float32)
    return jnp.cos(math.pi * (level_index[:, None] + 0.5) * level_index[None, :] / levels)

def poisson(divergence):
    levels = divergence.shape[2]
    level_table = cosine_table(levels)
    spectral = jnp.einsum('ijz,zm->mij', divergence, level_table, precision=HIGHEST)
    wave_x = 2.0 * jnp.cos(2.0 * math.pi * jnp.arange(NX).astype(jnp.float32) / NX) - 2.0
    wave_y = 2.0 * jnp.cos(2.0 * math.pi * jnp.arange(NY).astype(jnp.float32) / NY) - 2.0

    def solve_mode(operand):
        one_plane, mode_number = operand
        wave_z = 2.0 * jnp.cos(math.pi * mode_number.astype(jnp.float32) / levels) - 2.0
        eigenvalue = wave_x[:, None] + wave_y[None, :] + wave_z
        anchor = (mode_number == 0) & (jnp.arange(NX)[:, None] == 0) & (jnp.arange(NY)[None, :] == 0)
        safe_value = jnp.where(anchor, 1.0, eigenvalue)
        mode_values = jnp.fft.fft2(one_plane)
        solved = jnp.where(anchor, 0.0, mode_values / safe_value)
        return jnp.real(jnp.fft.ifft2(solved))
    modal = lax.map(solve_mode, (spectral, jnp.arange(levels).astype(jnp.int32)))
    weight = jnp.where(jnp.arange(levels) == 0, 1.0 / levels, 2.0 / levels)
    return jnp.einsum('mij,zm->ijz', modal, level_table * weight[None, :], precision=HIGHEST)

def to_boxes(grid_values):
    return grid_values.reshape(N_GX, BXD, N_GY, BYD).transpose(0, 2, 1, 3).reshape(BOXES)

def from_boxes(box_values):
    return box_values.reshape(N_GX, N_GY, BXD, BYD).transpose(0, 2, 1, 3).reshape(NBX, NBY)

def reference(velocity, theta, vapour, radius_sq, multiplicity, counts, pairing, destination):
    speed_x, speed_y, speed_z = (velocity[0], velocity[1], velocity[2])
    advected = [advect_one(values, speed_x, speed_y, speed_z) for values in (velocity[0], velocity[1], velocity[2], theta, vapour)]
    star_x = advected[0]
    star_y = advected[1]
    star_z = advected[2] + TIME_STEP * BUOYANCY * theta
    below_z = jnp.concatenate([jnp.zeros_like(star_z[..., :1]), star_z[..., :-1]], axis=-1)
    divergence = star_x - jnp.roll(star_x, 1, 0) + (star_y - jnp.roll(star_y, 1, 1)) + (star_z - below_z)
    pressure = poisson(divergence)
    step_east = jnp.roll(pressure, -1, 0) - pressure
    step_north = jnp.roll(pressure, -1, 1) - pressure
    step_up = jnp.concatenate([pressure[..., 1:], pressure[..., -1:]], axis=-1) - pressure
    velocity_new = jnp.stack([star_x - step_east, star_y - step_north, star_z - step_up])
    theta_new = advected[3]
    moist_field = advected[4]
    box_mean = to_boxes(moist_field.reshape(NBX, BW, NBY, BW, NZ).mean(axis=(1, 3, 4)))
    slot_index = jnp.arange(SLOTS)[:, None]
    live_weight = jnp.where(slot_index < counts[None, :], multiplicity, 0.0)
    grown_sq = radius_sq + GROWTH * jax.nn.softplus(box_mean)[None, :]
    mass_before = radius_sq * jnp.sqrt(radius_sq)
    mass_grown = grown_sq * jnp.sqrt(grown_sq)
    condensed = lax.optimization_barrier(jnp.sum(live_weight * (mass_grown - mass_before), axis=0))
    vapour_new = (moist_field.reshape(NBX, BW, NBY, BW, NZ) - CONDENSE * from_boxes(condensed)[:, None, :, None, None]).reshape(NX, NY, NZ)
    row_index = jnp.arange(BOXES)[:, None]
    partner = jnp.zeros_like(pairing).at[row_index, pairing].set(jnp.roll(pairing, -(SLOTS // 2), axis=1)).T
    other_grown = jnp.take_along_axis(grown_sq, partner, axis=0)
    other_live = jnp.take_along_axis(live_weight, partner, axis=0)
    other_mass = jnp.take_along_axis(mass_grown, partner, axis=0)
    radius_sum = jnp.sqrt(grown_sq) + jnp.sqrt(other_grown)
    collide_rate = radius_sum * radius_sum * jnp.abs(grown_sq - other_grown) * other_live
    mass_final = (mass_grown + COLLISION * collide_rate * other_mass) / (1.0 + COLLISION * collide_rate)
    carried_load = jnp.stack([live_weight, live_weight * mass_final, live_weight * mass_final * mass_final]).reshape(3, SLOTS * BOXES)
    flat_target = destination.reshape(SLOTS * BOXES)
    moments = jax.vmap(lambda line: jax.ops.segment_sum(line, flat_target, num_segments=BOXES))(carried_load) / SLOTS
    return (velocity_new, theta_new, vapour_new, moments)
```

```python
import functools
import math

import jax
import jax.numpy as jnp
import ml_dtypes
import numpy as np
from jax import lax
from jax.experimental import pallas as pl
from jax.experimental.pallas import tpu as pltpu
from jax.sharding import PartitionSpec as P

BW = 4
LANES = 128

TIME_STEP = 0.2
DIFFUSION = 0.05
BUOYANCY = 0.5
GROWTH = 0.5
COLLISION = 0.05
CONDENSE = 0.002

VMEM = pl.BlockSpec(memory_space=pltpu.VMEM)
PARAMS = pltpu.CompilerParams(vmem_limit_bytes=24 * 2**20)
NT = (((1,), (1,)), ((), ()))
TN = (((0,), (0,)), ((), ()))
NN = (((1,), (0,)), ((), ()))

KINDS = [(sx, sy) for sx in (-1, 0, 1) for sy in (-1, 0, 1) if (sx, sy) != (0, 0)]


def halves(table):
    high = table.astype(np.float32).astype(ml_dtypes.bfloat16)
    low = (table - high.astype(np.float64)).astype(np.float32).astype(ml_dtypes.bfloat16)
    return high, low


def split(value):
    high = value.astype(jnp.bfloat16)
    return high, (value - high.astype(jnp.float32)).astype(jnp.bfloat16)


def dot3(left, right, dims=NN):
    (lh, ll), (rh, rl) = left, right
    dot = functools.partial(
        lax.dot_general, dimension_numbers=dims, preferred_element_type=jnp.float32
    )
    return dot(lh, rh) + (dot(ll, rh) + dot(lh, rl))


def real_basis(length):
    position = np.arange(length)[:, None]
    column = np.arange(length)
    wave = np.where(column <= length // 2, column, column - length // 2)
    angle = 2.0 * np.pi * ((position * wave[None, :]) % length) / length
    table = np.where(column[None, :] <= length // 2, np.cos(angle), np.sin(angle))
    table = table * np.sqrt(2.0 / length)
    table[:, 0] *= np.sqrt(0.5)
    if length % 2 == 0:
        table[:, length // 2] *= np.sqrt(0.5)
    return table, -4.0 * np.sin(np.pi * wave / length) ** 2


class Plan:
    def __init__(self, grid_x, grid_y, span_x, span_y, levels, slots):
        self.gx, self.gy = grid_x, grid_y
        self.sx, self.sy, self.nz = span_x, span_y, levels
        self.nd = grid_x * grid_y
        self.per = levels // self.nd
        self.x4 = LANES // span_y
        self.xg = span_x // self.x4
        self.main = self.per * self.xg
        self.rows1 = self.main + 2
        self.rows2 = self.main + 3
        self.tx, self.ty = grid_x * span_x, grid_y * span_y
        self.bx, self.by = span_x // BW, span_y // BW
        self.boxes = self.bx * self.by
        self.slots = slots

    def tables(self):
        nd, per, nz = self.nd, self.per, self.nz
        z = np.arange(nz)
        cosine = np.cos(np.pi / nz * (((2 * z[:, None] + 1) * z[None, :]) % (4 * nz)) / 2.0)
        mode = (np.arange(nd)[None, :] * per + np.arange(per)[:, None]).reshape(-1)
        forward = cosine.T[mode]
        weight = np.where(np.arange(nz) == 0, 1.0, 2.0) / nz
        backward = forward * weight[mode][:, None]
        qx, ex = real_basis(self.tx)
        qy, ey = real_basis(self.ty)
        q1 = qx.reshape(self.gx, self.xg, self.x4, self.tx)
        q1 = q1.transpose(3, 2, 1, 0).reshape(self.tx, self.tx)
        w = np.einsum("byk,pq->bpyqk", qy.reshape(self.gy, self.sy, self.ty), np.eye(self.x4))
        w = w.reshape(self.gy * LANES, self.x4 * self.ty)
        ez = -4.0 * np.sin(np.pi * z / (2 * nz)) ** 2
        return forward, backward, q1, w, ex, ey, ez


def neighbours(count):
    first = [(i, i ^ 1) for i in range(count)]
    second = [(i, (i + 1) % count if i % 2 else (i - 1) % count) for i in range(count)]
    return first, second


def edges_kernel(plan, vel, theta, vapour, xa, xb, ya, yb):
    odd_x = lax.axis_index("gx") % 2 == 1
    odd_y = lax.axis_index("gy") % 2 == 1
    fields = [(vel, i) for i in range(3)] + [(theta, None), (vapour, None)]
    for f, (ref, i) in enumerate(fields):
        at = (lambda x, ref=ref, i=i: ref[x] if i is None else ref[i, x])
        first, last = at(0), at(plan.sx - 1)
        xa[f] = jnp.where(odd_x, first, last)
        xb[f] = jnp.where(odd_x, last, first)
        for x in range(plan.sx):
            if i is None:
                south, north = ref[x, 0:1], ref[x, plan.sy - 1 : plan.sy]
            else:
                south, north = ref[i, x, 0:1], ref[i, x, plan.sy - 1 : plan.sy]
            ya[f, x : x + 1] = jnp.where(odd_y, south, north)
            yb[f, x : x + 1] = jnp.where(odd_y, north, south)


def edge_masks(plan):
    row = lax.broadcasted_iota(jnp.int32, (plan.sy, plan.nz), 0)
    lane = lax.broadcasted_iota(jnp.int32, (plan.sy, plan.nz), 1)
    return row == 0, row == plan.sy - 1, lane == 0, lane == plan.nz - 1


def coefficients(u, v, w):
    half = 0.5 * TIME_STEP
    side = TIME_STEP * DIFFUSION
    return (
        side - half * u, side + half * u,
        side - half * v, side + half * v,
        side - half * w, side + half * w,
    )


def advect(c, east, west, north_row, south_row, coef, masks, plan):
    row0, row_last, lane0, lane_last = masks
    north = jnp.where(row_last, north_row, pltpu.roll(c, plan.sy - 1, 0))
    south = jnp.where(row0, south_row, pltpu.roll(c, 1, 0))
    upper = jnp.where(lane_last, c, pltpu.roll(c, plan.nz - 1, 1))
    lower = jnp.where(lane0, c, pltpu.roll(c, 1, 1))
    ce, cw, cn, cs, cu, cl = coef
    return (
        (1.0 - 6.0 * TIME_STEP * DIFFUSION) * c
        + (ce * east + cw * west)
        + (cn * north + cs * south)
        + (cu * upper + cl * lower)
    )


def side_planes(xa, xb, f):
    odd = lax.axis_index("gx") % 2 == 1
    return jnp.where(odd, xa[f], xb[f]), jnp.where(odd, xb[f], xa[f])


def side_rows(ya, yb, f):
    odd = lax.axis_index("gy") % 2 == 1
    return jnp.where(odd, ya[f], yb[f]), jnp.where(odd, yb[f], ya[f])


def wind_kernel(plan, vel, theta, xa, xb, ya, yb, fh, fl, star, out):
    masks = edge_masks(plan)
    table = (fh[...], fl[...])
    west_of, east_of, south_of, north_of = [], [], [], []
    for f in range(3):
        west, east = side_planes(xa, xb, f)
        south, north = side_rows(ya, yb, f)
        west_of.append(west)
        east_of.append(east)
        south_of.append(south)
        north_of.append(north)
    row0, _, lane0, _ = masks
    last_u = None
    slab = []
    last_rows = []
    for x in range(plan.sx):
        coef = coefficients(vel[0, x], vel[1, x], vel[2, x])
        s = []
        for f in range(3):
            west = vel[f, x - 1] if x else west_of[f]
            east = vel[f, x + 1] if x < plan.sx - 1 else east_of[f]
            s.append(
                advect(
                    vel[f, x], east, west, north_of[f][x : x + 1], south_of[f][x : x + 1],
                    coef, masks, plan,
                )
            )
        s[2] = s[2] + (TIME_STEP * BUOYANCY) * theta[x]
        for f in range(3):
            star[f, x] = s[f]
        div = s[0] if last_u is None else s[0] - last_u
        div = div + (s[1] - jnp.where(row0, 0.0, pltpu.roll(s[1], 1, 0)))
        div = div + (s[2] - jnp.where(lane0, 0.0, pltpu.roll(s[2], 1, 1)))
        last_u = s[0]
        last_rows.append(s[1][plan.sy - 1 : plan.sy])
        slab.append(div)
        if len(slab) == plan.x4:
            g = x // plan.x4
            modes = dot3(table, split(jnp.concatenate(slab, axis=0)), NT)
            for j in range(plan.per):
                out[pl.ds(j * plan.xg + g, plan.nd, stride=plan.rows1), :] = modes[
                    j * plan.nd : (j + 1) * plan.nd
                ]
            slab = []
    tiled_plane = jnp.concatenate([-last_u] * plan.x4, axis=0)
    row = lax.broadcasted_iota(jnp.int32, (plan.sy, plan.nz), 0)
    tiled_rows = []
    for p in range(plan.x4):
        block = jnp.zeros((plan.sy, plan.nz), jnp.float32)
        for g in range(plan.xg):
            block = jnp.where(row % plan.xg == g, -last_rows[g * plan.x4 + p], block)
        tiled_rows.append(block)
    extra = dot3(table, split(jnp.concatenate([tiled_plane] + tiled_rows, axis=0)), NT)
    lane = lax.broadcasted_iota(jnp.int32, (plan.nd, LANES), 1)
    plane_sum = jnp.zeros((plan.nd, LANES), jnp.float32)
    row_sum = jnp.zeros((plan.nd, LANES), jnp.float32)
    for j in range(plan.per):
        part = extra[j * plan.nd : (j + 1) * plan.nd]
        plane_sum = jnp.where(lane // plan.sy == j, part[:, :LANES], plane_sum)
        row_sum = jnp.where(lane % plan.sy // plan.xg == j, part[:, LANES:], row_sum)
    out[pl.ds(plan.main, plan.nd, stride=plan.rows1), :] = plane_sum
    out[pl.ds(plan.main + 1, plan.nd, stride=plan.rows1), :] = row_sum


def solve_kernel(plan, r, inverse, leave, wh, wl, th, tl, qh, ql, qth, qtl, out):
    gx, gy, per, xg, x4 = plan.gx, plan.gy, plan.per, plan.xg, plan.x4
    lane = lax.broadcasted_iota(jnp.int32, (gx, LANES), 1)
    first_lanes = lane < plan.sy
    first_rows = lane % plan.sy == 0
    step1, step2 = gy * plan.rows1, gy * plan.rows2

    def take(b, q):
        return r[pl.ds(b * plan.rows1 + q, gx, stride=step1), :]

    blocks = [[take(b, q) for q in range(plan.main)] for b in range(gy)]
    for b in range(gy):
        plane = pltpu.roll(take(b, plan.main), 1, 0)
        for j in range(per):
            moved = plane if j == 0 else pltpu.roll(plane, LANES - j * plan.sy, 1)
            blocks[b][j * xg] = blocks[b][j * xg] + jnp.where(first_lanes, moved, 0.0)
        rows = take(b, plan.main + 1)
        for q in range(plan.main):
            moved = rows if q == 0 else pltpu.roll(rows, LANES - q, 1)
            nb = (b + 1) % gy
            blocks[nb][q] = blocks[nb][q] + jnp.where(first_rows, moved, 0.0)
    grid = jnp.concatenate([jnp.concatenate(column, axis=0) for column in blocks], axis=1)
    in_y = dot3(split(grid), (wh[...], wl[...]))
    height = xg * gx

    def swap(value, outer, inner):
        return jnp.concatenate(
            [
                jnp.concatenate(
                    [
                        value[o * height : (o + 1) * height, i * plan.ty : (i + 1) * plan.ty]
                        for o in range(outer)
                    ],
                    axis=1,
                )
                for i in range(inner)
            ],
            axis=0,
        )

    spectral = dot3((qh[...], ql[...]), split(swap(in_y, per, x4)))
    solved = spectral * inverse[...]
    in_x = dot3((qth[...], qtl[...]), split(solved))
    grid = dot3(split(swap(in_x, x4, per)), (th[...], tl[...]))
    planes = [jnp.zeros((gx, LANES), jnp.float32) for _ in range(gy)]
    rows = [jnp.zeros((gx, LANES), jnp.float32) for _ in range(gy)]
    for b in range(gy):
        for q in range(plan.main):
            block = grid[q * gx : (q + 1) * gx, b * LANES : (b + 1) * LANES]
            out[pl.ds(b * plan.rows2 + q, gx, stride=step2), :] = block
            moved = jnp.where(first_rows, block, 0.0)
            nb = (b - 1) % gy
            rows[nb] = rows[nb] + (moved if q == 0 else pltpu.roll(moved, q, 1))
            if q % xg == 0:
                j = q // xg
                moved = jnp.where(first_lanes, block, 0.0)
                planes[b] = planes[b] + (moved if j == 0 else pltpu.roll(moved, j * plan.sy, 1))
    for b in range(gy):
        out[pl.ds(b * plan.rows2 + plan.main, gx, stride=step2), :] = pltpu.roll(
            planes[b], gx - 1, 0
        )
        out[pl.ds(b * plan.rows2 + plan.main + 1, gx, stride=step2), :] = rows[b]
    out[pl.ds(plan.main + 2, plan.nd, stride=plan.rows2), :] = leave[...]


def project_kernel(plan, r, star, stay, bh, bl, place, vel_new, moments, scratch):
    nd, per, xg, x4, sy, sx = plan.nd, plan.per, plan.xg, plan.x4, plan.sy, plan.sx
    table = (bh[...], bl[...])
    lane = lax.broadcasted_iota(jnp.int32, (nd, LANES), 1)

    def take(q):
        return r[pl.ds(q, nd, stride=plan.rows2), :]

    planes, rows = take(plan.main), take(plan.main + 1)
    wide = jnp.concatenate(
        [
            jnp.concatenate([jnp.where(lane // sy == j, planes, 0.0) for j in range(per)], axis=0),
            jnp.concatenate(
                [jnp.where(lane % sy // xg == j, rows, 0.0) for j in range(per)], axis=0
            ),
        ],
        axis=1,
    )
    extra = dot3(split(wide), table, TN)
    beyond = extra[0:sy]
    for j in range(1, per):
        beyond = beyond + extra[j * sy : (j + 1) * sy]
    scratch[...] = extra[LANES:]
    row = lax.broadcasted_iota(jnp.int32, (sy, plan.nz), 0)
    level = lax.broadcasted_iota(jnp.int32, (sy, plan.nz), 1)
    pressure = []
    for g in range(xg):
        modes = jnp.concatenate([take(j * xg + g) for j in range(per)], axis=0)
        slab = dot3(split(modes), table, TN)
        pressure += [slab[p * sy : (p + 1) * sy] for p in range(x4)]
    pressure.append(beyond)
    for x in range(sx):
        here = pressure[x]
        g, p = x // x4, x % x4
        last = scratch[p * sy + g : p * sy + g + 1]
        for j in range(1, per):
            last = last + scratch[p * sy + j * xg + g : p * sy + j * xg + g + 1]
        north = jnp.where(row == sy - 1, last, pltpu.roll(here, sy - 1, 0))
        upper = jnp.where(level == plan.nz - 1, here, pltpu.roll(here, plan.nz - 1, 1))
        vel_new[0, x] = star[0, x] - (pressure[x + 1] - here)
        vel_new[1, x] = star[1, x] - (north - here)
        vel_new[2, x] = star[2, x] - (upper - here)
    came = jnp.sum(take(plan.main + 2), axis=0, keepdims=True)
    load = lax.broadcasted_iota(jnp.int32, (8, LANES), 0)
    at = lax.broadcasted_iota(jnp.int32, (8, LANES), 1)
    width = payload_width(plan)
    loads = jnp.where(at // width == load, came, 0.0)
    total = stay[...] + lax.dot_general(
        loads, place[...], NN, precision=lax.Precision.HIGHEST, preferred_element_type=jnp.float32
    )
    moments[...] = total[:3, : plan.boxes] * (1.0 / plan.slots)


def payload_width(plan):
    return 2 * plan.by + 2 * plan.bx + 4


def droplet_tables(plan):
    bx, by, boxes = plan.bx, plan.by, plan.boxes
    width = payload_width(plan)
    lane_of = {}
    kind_of = np.full((LANES,), -1)
    place = np.zeros((LANES, LANES), np.float32)
    for k, (sx, sy) in enumerate(KINDS):
        xs = range(bx) if sx == 0 else [0 if sx > 0 else bx - 1]
        ys = range(by) if sy == 0 else [0 if sy > 0 else by - 1]
        for x in xs:
            for y in ys:
                lane_of[k, x, y] = len(lane_of)
    assert len(lane_of) == width and 3 * width <= LANES
    for (k, x, y), at in lane_of.items():
        for load in range(3):
            kind_of[load * width + at] = k
            place[load * width + at, x * by + y] = 1.0
    here = np.zeros((9 * boxes, LANES), np.float32)
    away = np.zeros((3, 9 * boxes, LANES), np.float32)
    for dx in (-1, 0, 1):
        for dy in (-1, 0, 1):
            code = (dx + 1) * 3 + dy + 1
            for x in range(bx):
                for y in range(by):
                    line = code * boxes + x * by + y
                    sx = (x + dx) // bx
                    sy = (y + dy) // by
                    tx, ty = (x + dx) % bx, (y + dy) % by
                    if (sx, sy) == (0, 0):
                        here[line, tx * by + ty] = 1.0
                    else:
                        at = lane_of[KINDS.index((sx, sy)), tx, ty]
                        for load in range(3):
                            away[load, line, load * width + at] = 1.0
    return here, away, place, kind_of


def scalar_kernel(
    plan, vel, theta, vapour, xa, xb, ya, yb, drops, order, here, away, target,
    theta_new, vapour_new, stay, leave, moist,
):
    masks = edge_masks(plan)
    bx, by, boxes = plan.bx, plan.by, plan.boxes
    edges = []
    for f in (3, 4):
        west, east = side_planes(xa, xb, f)
        south, north = side_rows(ya, yb, f)
        edges.append((west, east, south, north))
    sums = []
    total = None
    for x in range(plan.sx):
        coef = coefficients(vel[0, x], vel[1, x], vel[2, x])
        for ref, new, (west, east, south, north) in (
            (theta, theta_new, edges[0]),
            (vapour, moist, edges[1]),
        ):
            moved = advect(
                ref[x],
                ref[x + 1] if x < plan.sx - 1 else east,
                ref[x - 1] if x else west,
                north[x : x + 1], south[x : x + 1], coef, masks, plan,
            )
            new[x] = moved
        total = moved if x % BW == 0 else total + moved
        if x % BW == BW - 1:
            sums.append(jnp.sum(total, axis=1, keepdims=True))
    exact = functools.partial(
        lax.dot_general, dimension_numbers=NN, precision=lax.Precision.HIGHEST,
        preferred_element_type=jnp.float32,
    )
    gather_y = (
        lax.broadcasted_iota(jnp.int32, (by, plan.sy), 1) // BW
        == lax.broadcasted_iota(jnp.int32, (by, plan.sy), 0)
    ).astype(jnp.float32)
    spread_y = (
        lax.broadcasted_iota(jnp.int32, (plan.sy, by), 0) // BW
        == lax.broadcasted_iota(jnp.int32, (plan.sy, by), 1)
    ).astype(jnp.float32)
    means = jnp.concatenate(
        [exact(gather_y, jnp.broadcast_to(s, (plan.sy, LANES))) for s in sums], axis=0
    ) * (1.0 / (BW * BW * plan.nz))
    softplus = jnp.maximum(means, 0.0) + jnp.log(1.0 + jnp.exp(-jnp.abs(means)))
    index = order[...]

    def gather(value):
        return jnp.take_along_axis(value, index, axis=1, mode="promise_in_bounds")

    radius_sq = gather(drops[0])
    live = gather(drops[1])
    code = gather(drops[2])
    grown_sq = radius_sq + GROWTH * softplus
    root = jnp.sqrt(grown_sq)
    mass = grown_sq * root
    lane = lax.broadcasted_iota(jnp.int32, (boxes, LANES), 1)
    own = lane < plan.slots
    condensed = jnp.sum(
        jnp.where(own, live * (mass - radius_sq * jnp.sqrt(radius_sq)), 0.0),
        axis=1, keepdims=True,
    )
    condensed = jnp.broadcast_to(condensed, (boxes, LANES))
    for big in range(bx):
        less = CONDENSE * exact(spread_y, condensed[big * by : (big + 1) * by])
        for x in range(big * BW, (big + 1) * BW):
            vapour_new[x] = moist[x] - less

    def partner(value):
        return pltpu.roll(value, LANES - plan.slots, 1)

    other_grown, other_root, other_mass = partner(grown_sq), partner(root), partner(mass)
    both = root + other_root
    rate = both * both * jnp.abs(grown_sq - other_grown) * partner(live)
    final = (mass + COLLISION * rate * other_mass) / (1.0 + COLLISION * rate)
    weight = jnp.where(own, live, 0.0)
    loads = (weight, weight * final, weight * final * final)
    parts = [[], [], []]
    for direction in range(9):
        chosen = code == float(direction)
        for k in range(3):
            parts[k].append(
                jnp.sum(jnp.where(chosen, loads[k], 0.0), axis=1, keepdims=True)
            )
    payload = jnp.zeros((1, LANES), jnp.float32)
    stays = jnp.zeros((8, LANES), jnp.float32)
    line = lax.broadcasted_iota(jnp.int32, (8, LANES), 0)
    for k in range(3):
        column = jnp.concatenate(parts[k], axis=0)
        payload = payload + jnp.sum(column * away[k], axis=0, keepdims=True)
        stays = jnp.where(line == k, jnp.sum(column * here[...], axis=0, keepdims=True), stays)
    stay[...] = stays
    leave[...] = payload * target[...]


def call(body, outs, args, flops, scratch=()):
    moved = sum(a.size * a.dtype.itemsize for a in args)
    moved += sum(math.prod(o) * 4 for o in outs)
    return pl.pallas_call(
        body,
        out_shape=[jax.ShapeDtypeStruct(o, jnp.float32) for o in outs],
        in_specs=[VMEM] * len(args),
        out_specs=[VMEM] * len(outs),
        scratch_shapes=list(scratch),
        compiler_params=PARAMS,
        cost_estimate=pl.CostEstimate(flops=flops, bytes_accessed=moved, transcendentals=0),
    )(*args)


def swap(block, axis):
    first, second = neighbours(lax.axis_size(axis))
    return (lambda a, b: (lax.ppermute(a, axis, first), lax.ppermute(b, axis, second)))(*block)


def exchange(chunks, plan, rows):
    flat = chunks.reshape(plan.nd, 1, rows * LANES)
    flat = lax.all_to_all(flat, ("gx", "gy"), split_axis=0, concat_axis=0, tiled=True)
    return flat.reshape(plan.nd * rows, LANES)


def shards(velocity, theta, vapour, radius_sq, multiplicity, counts, pairing, destination):
    span_x, span_y, levels = theta.shape
    slots = radius_sq.shape[0]
    plan = Plan(lax.axis_size("gx"), lax.axis_size("gy"), span_x, span_y, levels, slots)
    rank_x, rank_y = lax.axis_index("gx"), lax.axis_index("gy")
    rank = rank_x * plan.gy + rank_y
    forward, backward, q1, w, ex, ey, ez = plan.tables()
    here, away, place, kind_of = droplet_tables(plan)
    block = (span_x, span_y, levels)
    cells = math.prod(block)

    plane, rows = (5, span_y, levels), (5, span_x, levels)
    xa, xb, ya, yb = call(
        functools.partial(edges_kernel, plan),
        (plane, plane, rows, rows), (velocity, theta, vapour), cells,
    )
    xa, xb = swap((xa, xb), "gx")
    ya, yb = swap((ya, yb), "gy")

    box = jnp.arange(plan.boxes)
    source_x = rank_x * plan.bx + box // plan.by
    source_y = rank_y * plan.by + box % plan.by
    device, local = destination // plan.boxes, destination % plan.boxes
    target_x = device // plan.gy * plan.bx + local // plan.by
    target_y = device % plan.gy * plan.by + local % plan.by
    offset_x = (target_x - source_x[None, :] + 1) % (plan.bx * plan.gx)
    offset_y = (target_y - source_y[None, :] + 1) % (plan.by * plan.gy)
    live = jnp.where(jnp.arange(slots)[:, None] < counts[None, :], multiplicity, 0.0)
    drops = jnp.stack([radius_sq, live, (offset_x * 3 + offset_y).astype(jnp.float32)])
    drops = jnp.pad(jnp.swapaxes(drops, 1, 2), ((0, 0), (0, 0), (0, LANES - slots)))
    order = jnp.concatenate([pairing, jnp.roll(pairing, slots // 2, axis=1)], axis=1)
    every = jnp.arange(plan.nd)
    target = jnp.zeros((plan.nd, LANES), jnp.float32)
    for k, (sx, sy) in enumerate(KINDS):
        to = (rank_x + sx) % plan.gx * plan.gy + (rank_y + sy) % plan.gy
        target = target + ((every == to)[:, None] & (kind_of == k)[None, :]).astype(jnp.float32)

    star, chunks = call(
        functools.partial(wind_kernel, plan),
        ((3,) + block, (plan.nd * plan.rows1, LANES)),
        (velocity, theta, xa, xb, ya, yb) + halves(forward),
        100 * cells,
    )
    spectral = exchange(chunks, plan, plan.rows1)

    theta_new, vapour_new, stay, leave = call(
        functools.partial(scalar_kernel, plan),
        (block, block, (8, LANES), (plan.nd, LANES)),
        (velocity, theta, vapour, xa, xb, ya, yb, drops, order, here, away, target),
        100 * cells,
        (pltpu.VMEM(block, jnp.float32),),
    )

    modes = lax.dynamic_slice(jnp.asarray(ez, jnp.float32), (rank * plan.per,), (plan.per,))
    eigen = (
        jnp.asarray(ex, jnp.float32)[:, None, None]
        + jnp.asarray(ey, jnp.float32)[None, None, :]
        + modes[None, :, None]
    ).reshape(plan.tx, plan.per * plan.ty)
    inverse = jnp.where(eigen == 0.0, 0.0, 1.0 / jnp.where(eigen == 0.0, 1.0, eigen))
    (chunks,) = call(
        functools.partial(solve_kernel, plan),
        ((plan.nd * plan.rows2, LANES),),
        (spectral, inverse, leave) + halves(w) + halves(w.T) + halves(q1) + halves(q1.T),
        1000 * cells,
    )
    modal = exchange(chunks, plan, plan.rows2)

    velocity_new, moments = call(
        functools.partial(project_kernel, plan),
        ((3,) + block, (3, plan.boxes)),
        (modal, star, stay) + halves(backward) + (place,),
        100 * cells,
        (pltpu.VMEM((LANES, levels), jnp.float32),),
    )
    return (velocity_new, theta_new, vapour_new, moments)


def solution(mesh):
    placed = (
        P(None, "gx", "gy", None),
        P("gx", "gy", None),
        P("gx", "gy", None),
        P(None, ("gx", "gy")),
        P(None, ("gx", "gy")),
        P(("gx", "gy")),
        P(("gx", "gy"), None),
        P(None, ("gx", "gy")),
    )
    return jax.shard_map(
        shards,
        mesh=mesh,
        in_specs=placed,
        out_specs=(
            P(None, "gx", "gy", None),
            P("gx", "gy", None),
            P("gx", "gy", None),
            P(None, ("gx", "gy")),
        ),
        check_vma=False,
    )
```

```python
import functools
import math

import jax
import jax.numpy as jnp
import ml_dtypes
import numpy as np
from jax import lax
from jax.experimental import pallas as pl
from jax.experimental.pallas import tpu as pltpu
from jax.sharding import PartitionSpec as P

BW = 4
LANES = 128

EDGE_LIMIT = 55040 * 2**10

TIME_STEP = 0.2
DIFFUSION = 0.05
BUOYANCY = 0.5
GROWTH = 0.5
COLLISION = 0.05
CONDENSE = 0.002

VMEM = pl.BlockSpec(memory_space=pltpu.VMEM)
HBM = pl.BlockSpec(memory_space=pltpu.HBM)
NT = (((1,), (1,)), ((), ()))
TN = (((0,), (0,)), ((), ()))
NN = (((1,), (0,)), ((), ()))

KINDS = [(sx, sy) for sx in (-1, 0, 1) for sy in (-1, 0, 1) if (sx, sy) != (0, 0)]


def halves(table):
    high = table.astype(np.float32).astype(ml_dtypes.bfloat16)
    low = (table - high.astype(np.float64)).astype(np.float32).astype(ml_dtypes.bfloat16)
    return high, low


def split(value):
    high = value.astype(jnp.bfloat16)
    return high, (value - high.astype(jnp.float32)).astype(jnp.bfloat16)


def dot3(left, right, dims=NN):
    (lh, ll), (rh, rl) = left, right
    dot = functools.partial(
        lax.dot_general, dimension_numbers=dims, preferred_element_type=jnp.float32
    )
    return dot(lh, rh) + (dot(ll, rh) + dot(lh, rl))


def real_basis(length):
    position = np.arange(length)[:, None]
    column = np.arange(length)
    wave = np.where(column <= length // 2, column, column - length // 2)
    angle = 2.0 * np.pi * ((position * wave[None, :]) % length) / length
    table = np.where(column[None, :] <= length // 2, np.cos(angle), np.sin(angle))
    table = table * np.sqrt(2.0 / length)
    table[:, 0] *= np.sqrt(0.5)
    if length % 2 == 0:
        table[:, length // 2] *= np.sqrt(0.5)
    return table, -4.0 * np.sin(np.pi * wave / length) ** 2


class Plan:
    def __init__(self, grid_x, grid_y, span_x, span_y, levels, slots):
        self.gx, self.gy = grid_x, grid_y
        self.sx, self.sy, self.nz = span_x, span_y, levels
        self.nd = grid_x * grid_y
        self.per = levels // self.nd
        self.x4 = LANES // span_y
        self.xg = span_x // self.x4
        self.main = self.per * self.xg
        self.rows1 = self.main + 2
        self.rows2 = self.main + 3
        self.tx, self.ty = grid_x * span_x, grid_y * span_y
        self.bx, self.by = span_x // BW, span_y // BW
        self.boxes = self.bx * self.by
        self.slots = slots

    def tables(self):
        nd, per, nz = self.nd, self.per, self.nz
        z = np.arange(nz)
        cosine = np.cos(np.pi / nz * (((2 * z[:, None] + 1) * z[None, :]) % (4 * nz)) / 2.0)
        mode = (np.arange(nd)[None, :] * per + np.arange(per)[:, None]).reshape(-1)
        forward = cosine.T[mode]
        weight = np.where(np.arange(nz) == 0, 1.0, 2.0) / nz
        backward = forward * weight[mode][:, None]
        qx, ex = real_basis(self.tx)
        qy, ey = real_basis(self.ty)
        q1 = qx.reshape(self.gx, self.xg, self.x4, self.tx)
        q1 = q1.transpose(3, 2, 1, 0).reshape(self.tx, self.tx)
        ez = -4.0 * np.sin(np.pi * z / (2 * nz)) ** 2
        return forward, backward, q1, qy, ex, ey, ez


def neighbours(count):
    first = [(i, i ^ 1) for i in range(count)]
    second = [(i, (i + 1) % count if i % 2 else (i - 1) % count) for i in range(count)]
    return first, second


def copy_all(copies):
    for copy in copies:
        copy.start()
    for copy in copies:
        copy.wait()


def plane_copies(vel, theta, vapour, x, out, sems):
    return [
        pltpu.make_async_copy(vel.at[:, x], out.at[0:3], sems.at[0]),
        pltpu.make_async_copy(theta.at[x], out.at[3], sems.at[1]),
        pltpu.make_async_copy(vapour.at[x], out.at[4], sems.at[2]),
    ]


def far_kernel(plan, vel, theta, vapour, xb, sems):
    odd = lax.axis_index("gx") % 2
    copy_all(plane_copies(vel, theta, vapour, (plan.sx - 1) * odd, xb, sems))


def near_kernel(plan, vel, theta, vapour, after, xa, ya, yb, south, north, sems):
    odd_x = lax.axis_index("gx") % 2
    odd_y = lax.axis_index("gy") % 2 == 1
    tile = south.shape[2]
    copies = plane_copies(vel, theta, vapour, (plan.sx - 1) * (1 - odd_x), xa, sems.at[2])
    for side, (out, y) in enumerate(((south, 0), (north, plan.sy - tile))):
        copies += [
            pltpu.make_async_copy(vel.at[:, :, y : y + tile], out.at[0:3], sems.at[side, 0]),
            pltpu.make_async_copy(theta.at[:, y : y + tile], out.at[3], sems.at[side, 1]),
            pltpu.make_async_copy(vapour.at[:, y : y + tile], out.at[4], sems.at[side, 2]),
        ]
    copy_all(copies)
    for f in range(5):
        low = jnp.concatenate([south[f, x, 0:1] for x in range(plan.sx)], axis=0)
        high = jnp.concatenate([north[f, x, tile - 1 : tile] for x in range(plan.sx)], axis=0)
        ya[f] = jnp.where(odd_y, low, high)
        yb[f] = jnp.where(odd_y, high, low)


def edge_masks(plan):
    row = lax.broadcasted_iota(jnp.int32, (plan.sy, plan.nz), 0)
    lane = lax.broadcasted_iota(jnp.int32, (plan.sy, plan.nz), 1)
    return row == 0, row == plan.sy - 1, lane == 0, lane == plan.nz - 1


def coefficients(u, v, w):
    half = 0.5 * TIME_STEP
    side = TIME_STEP * DIFFUSION
    return (
        side - half * u, side + half * u,
        side - half * v, side + half * v,
        side - half * w, side + half * w,
    )


def advect(c, east, west, north_row, south_row, coef, masks, plan):
    row0, row_last, lane0, lane_last = masks
    north = jnp.where(row_last, north_row, pltpu.roll(c, plan.sy - 1, 0))
    south = jnp.where(row0, south_row, pltpu.roll(c, 1, 0))
    upper = jnp.where(lane_last, c, pltpu.roll(c, plan.nz - 1, 1))
    lower = jnp.where(lane0, c, pltpu.roll(c, 1, 1))
    ce, cw, cn, cs, cu, cl = coef
    return (
        (1.0 - 6.0 * TIME_STEP * DIFFUSION) * c
        + (ce * east + cw * west)
        + (cn * north + cs * south)
        + (cu * upper + cl * lower)
    )


def side_planes(xa, xb, f):
    odd = lax.axis_index("gx") % 2 == 1
    return jnp.where(odd, xa[f], xb[f]), jnp.where(odd, xb[f], xa[f])


def side_rows(ya, yb, f):
    odd = lax.axis_index("gy") % 2 == 1
    return jnp.where(odd, ya[f], yb[f]), jnp.where(odd, yb[f], ya[f])


def wind_kernel(plan, vel, theta, xa, xb, ya, yb, fh, fl, star, out):
    masks = edge_masks(plan)
    table = (fh[...], fl[...])
    west_of, east_of, south_of, north_of = [], [], [], []
    for f in range(3):
        west, east = side_planes(xa, xb, f)
        south, north = side_rows(ya, yb, f)
        west_of.append(west)
        east_of.append(east)
        south_of.append(south)
        north_of.append(north)
    row0, _, lane0, _ = masks
    last_u = None
    slab = []
    last_rows = []
    for x in range(plan.sx):
        coef = coefficients(vel[0, x], vel[1, x], vel[2, x])
        s = []
        for f in range(3):
            west = vel[f, x - 1] if x else west_of[f]
            east = vel[f, x + 1] if x < plan.sx - 1 else east_of[f]
            s.append(
                advect(
                    vel[f, x], east, west, north_of[f][x : x + 1], south_of[f][x : x + 1],
                    coef, masks, plan,
                )
            )
        s[2] = s[2] + (TIME_STEP * BUOYANCY) * theta[x]
        for f in range(3):
            star[f, x] = s[f]
        div = s[0] if last_u is None else s[0] - last_u
        div = div + (s[1] - jnp.where(row0, 0.0, pltpu.roll(s[1], 1, 0)))
        div = div + (s[2] - jnp.where(lane0, 0.0, pltpu.roll(s[2], 1, 1)))
        last_u = s[0]
        last_rows.append(s[1][plan.sy - 1 : plan.sy])
        slab.append(div)
        if len(slab) == plan.x4:
            g = x // plan.x4
            modes = dot3(table, split(jnp.concatenate(slab, axis=0)), NT)
            for j in range(plan.per):
                out[pl.ds(j * plan.xg + g, plan.nd, stride=plan.rows1), :] = modes[
                    j * plan.nd : (j + 1) * plan.nd
                ]
            slab = []
    tiled_plane = jnp.concatenate([-last_u] * plan.x4, axis=0)
    row = lax.broadcasted_iota(jnp.int32, (plan.sy, plan.nz), 0)
    tiled_rows = []
    for p in range(plan.x4):
        block = jnp.zeros((plan.sy, plan.nz), jnp.float32)
        for g in range(plan.xg):
            block = jnp.where(row % plan.xg == g, -last_rows[g * plan.x4 + p], block)
        tiled_rows.append(block)
    extra = dot3(table, split(jnp.concatenate([tiled_plane] + tiled_rows, axis=0)), NT)
    lane = lax.broadcasted_iota(jnp.int32, (plan.nd, LANES), 1)
    plane_sum = jnp.zeros((plan.nd, LANES), jnp.float32)
    row_sum = jnp.zeros((plan.nd, LANES), jnp.float32)
    for j in range(plan.per):
        part = extra[j * plan.nd : (j + 1) * plan.nd]
        plane_sum = jnp.where(lane // plan.sy == j, part[:, :LANES], plane_sum)
        row_sum = jnp.where(lane % plan.sy // plan.xg == j, part[:, LANES:], row_sum)
    out[pl.ds(plan.main, plan.nd, stride=plan.rows1), :] = plane_sum
    out[pl.ds(plan.main + 1, plan.nd, stride=plan.rows1), :] = row_sum


def solve_kernel(plan, r, inverse, leave, qy, qx, out, wide):
    gx, gy, per, xg, x4 = plan.gx, plan.gy, plan.per, plan.xg, plan.x4
    lane = lax.broadcasted_iota(jnp.int32, (gx, LANES), 1)
    first_lanes = lane < plan.sy
    first_rows = lane % plan.sy == 0
    step1, step2 = gy * plan.rows1, gy * plan.rows2

    for part in range(2):
        wide[part] = jnp.zeros(wide.shape[1:], wide.dtype)
        for b in range(gy):
            for p in range(x4):
                at = b * LANES + p * plan.sy
                wide[part, at : at + plan.sy, p * plan.ty : (p + 1) * plan.ty] = qy[
                    part, b * plan.sy : (b + 1) * plan.sy
                ]
    table_y = (wide[0], wide[1])

    def take(b, q):
        return r[pl.ds(b * plan.rows1 + q, gx, stride=step1), :]

    blocks = [[take(b, q) for q in range(plan.main)] for b in range(gy)]
    for b in range(gy):
        plane = pltpu.roll(take(b, plan.main), 1, 0)
        for j in range(per):
            moved = plane if j == 0 else pltpu.roll(plane, LANES - j * plan.sy, 1)
            blocks[b][j * xg] = blocks[b][j * xg] + jnp.where(first_lanes, moved, 0.0)
        rows = take(b, plan.main + 1)
        for q in range(plan.main):
            moved = rows if q == 0 else pltpu.roll(rows, LANES - q, 1)
            nb = (b + 1) % gy
            blocks[nb][q] = blocks[nb][q] + jnp.where(first_rows, moved, 0.0)
    grid = jnp.concatenate([jnp.concatenate(column, axis=0) for column in blocks], axis=1)
    in_y = dot3(split(grid), table_y)
    height = xg * gx

    def swap(value, outer, inner):
        return jnp.concatenate(
            [
                jnp.concatenate(
                    [
                        value[o * height : (o + 1) * height, i * plan.ty : (i + 1) * plan.ty]
                        for o in range(outer)
                    ],
                    axis=1,
                )
                for i in range(inner)
            ],
            axis=0,
        )

    spectral = dot3((qx[0], qx[1]), split(swap(in_y, per, x4)))
    solved = spectral * inverse[...]
    in_x = dot3((qx[2], qx[3]), split(solved))
    grid = dot3(split(swap(in_x, x4, per)), table_y, NT)
    planes = [jnp.zeros((gx, LANES), jnp.float32) for _ in range(gy)]
    rows = [jnp.zeros((gx, LANES), jnp.float32) for _ in range(gy)]
    for b in range(gy):
        for q in range(plan.main):
            block = grid[q * gx : (q + 1) * gx, b * LANES : (b + 1) * LANES]
            out[pl.ds(b * plan.rows2 + q, gx, stride=step2), :] = block
            moved = jnp.where(first_rows, block, 0.0)
            nb = (b - 1) % gy
            rows[nb] = rows[nb] + (moved if q == 0 else pltpu.roll(moved, q, 1))
            if q % xg == 0:
                j = q // xg
                moved = jnp.where(first_lanes, block, 0.0)
                planes[b] = planes[b] + (moved if j == 0 else pltpu.roll(moved, j * plan.sy, 1))
    for b in range(gy):
        out[pl.ds(b * plan.rows2 + plan.main, gx, stride=step2), :] = pltpu.roll(
            planes[b], gx - 1, 0
        )
        out[pl.ds(b * plan.rows2 + plan.main + 1, gx, stride=step2), :] = rows[b]
    out[pl.ds(plan.main + 2, plan.nd, stride=plan.rows2), :] = leave[...]


def project_kernel(plan, r, star, stay, bh, bl, place, vel_new, moments, scratch):
    nd, per, xg, x4, sy, sx = plan.nd, plan.per, plan.xg, plan.x4, plan.sy, plan.sx
    table = (bh[...], bl[...])
    lane = lax.broadcasted_iota(jnp.int32, (nd, LANES), 1)

    def take(q):
        return r[pl.ds(q, nd, stride=plan.rows2), :]

    planes, rows = take(plan.main), take(plan.main + 1)
    wide = jnp.concatenate(
        [
            jnp.concatenate([jnp.where(lane // sy == j, planes, 0.0) for j in range(per)], axis=0),
            jnp.concatenate(
                [jnp.where(lane % sy // xg == j, rows, 0.0) for j in range(per)], axis=0
            ),
        ],
        axis=1,
    )
    extra = dot3(split(wide), table, TN)
    beyond = extra[0:sy]
    for j in range(1, per):
        beyond = beyond + extra[j * sy : (j + 1) * sy]
    scratch[...] = extra[LANES:]
    row = lax.broadcasted_iota(jnp.int32, (sy, plan.nz), 0)
    level = lax.broadcasted_iota(jnp.int32, (sy, plan.nz), 1)
    pressure = []
    for g in range(xg):
        modes = jnp.concatenate([take(j * xg + g) for j in range(per)], axis=0)
        slab = dot3(split(modes), table, TN)
        pressure += [slab[p * sy : (p + 1) * sy] for p in range(x4)]
    pressure.append(beyond)
    for x in range(sx):
        here = pressure[x]
        g, p = x // x4, x % x4
        last = scratch[p * sy + g : p * sy + g + 1]
        for j in range(1, per):
            last = last + scratch[p * sy + j * xg + g : p * sy + j * xg + g + 1]
        north = jnp.where(row == sy - 1, last, pltpu.roll(here, sy - 1, 0))
        upper = jnp.where(level == plan.nz - 1, here, pltpu.roll(here, plan.nz - 1, 1))
        vel_new[0, x] = star[0, x] - (pressure[x + 1] - here)
        vel_new[1, x] = star[1, x] - (north - here)
        vel_new[2, x] = star[2, x] - (upper - here)
    came = jnp.sum(take(plan.main + 2), axis=0, keepdims=True)
    load = lax.broadcasted_iota(jnp.int32, (8, LANES), 0)
    at = lax.broadcasted_iota(jnp.int32, (8, LANES), 1)
    width = payload_width(plan)
    loads = jnp.where(at // width == load, came, 0.0)
    total = stay[...] + lax.dot_general(
        loads, place[...], NN, precision=lax.Precision.HIGHEST, preferred_element_type=jnp.float32
    )
    moments[...] = total[:3, : plan.boxes] * (1.0 / plan.slots)


def payload_width(plan):
    return 2 * plan.by + 2 * plan.bx + 4


def droplet_tables(plan):
    bx, by, boxes = plan.bx, plan.by, plan.boxes
    width = payload_width(plan)
    lane_of = {}
    kind_of = np.full((LANES,), -1)
    place = np.zeros((LANES, LANES), np.float32)
    for k, (sx, sy) in enumerate(KINDS):
        xs = range(bx) if sx == 0 else [0 if sx > 0 else bx - 1]
        ys = range(by) if sy == 0 else [0 if sy > 0 else by - 1]
        for x in xs:
            for y in ys:
                lane_of[k, x, y] = len(lane_of)
    assert len(lane_of) == width and max(3 * width, boxes + width) <= LANES
    for (k, x, y), at in lane_of.items():
        for load in range(3):
            kind_of[load * width + at] = k
            place[load * width + at, x * by + y] = 1.0
    goes = np.zeros((9 * boxes, LANES), np.float32)
    for dx in (-1, 0, 1):
        for dy in (-1, 0, 1):
            code = (dx + 1) * 3 + dy + 1
            for x in range(bx):
                for y in range(by):
                    line = code * boxes + x * by + y
                    sx = (x + dx) // bx
                    sy = (y + dy) // by
                    tx, ty = (x + dx) % bx, (y + dy) % by
                    if (sx, sy) == (0, 0):
                        goes[line, tx * by + ty] = 1.0
                    else:
                        goes[line, boxes + lane_of[KINDS.index((sx, sy)), tx, ty]] = 1.0
    return goes, place, kind_of[None].astype(np.int32)


def quotient(value, divisor):
    if divisor & (divisor - 1) == 0:
        return value >> (divisor.bit_length() - 1), value & (divisor - 1)
    return lax.div(value, divisor), lax.rem(value, divisor)


def scalar_kernel(
    plan, vel, theta, vapour, xa, xb, ya, yb, radius, multiplicity, counts, pairing,
    destination, goes, kind, theta_new, vapour_new, stay, leave, moist,
):
    masks = edge_masks(plan)
    bx, by, boxes = plan.bx, plan.by, plan.boxes
    edges = []
    for f in (3, 4):
        west, east = side_planes(xa, xb, f)
        south, north = side_rows(ya, yb, f)
        edges.append((west, east, south, north))
    sums = []
    total = None
    for x in range(plan.sx):
        coef = coefficients(vel[0, x], vel[1, x], vel[2, x])
        for ref, new, (west, east, south, north) in (
            (theta, theta_new, edges[0]),
            (vapour, moist, edges[1]),
        ):
            moved = advect(
                ref[x],
                ref[x + 1] if x < plan.sx - 1 else east,
                ref[x - 1] if x else west,
                north[x : x + 1], south[x : x + 1], coef, masks, plan,
            )
            new[x] = moved
        total = moved if x % BW == 0 else total + moved
        if x % BW == BW - 1:
            sums.append(jnp.sum(total, axis=1, keepdims=True))
    exact = functools.partial(
        lax.dot_general, dimension_numbers=NN, precision=lax.Precision.HIGHEST,
        preferred_element_type=jnp.float32,
    )
    gather_y = (
        lax.broadcasted_iota(jnp.int32, (by, plan.sy), 1) // BW
        == lax.broadcasted_iota(jnp.int32, (by, plan.sy), 0)
    ).astype(jnp.float32)
    spread_y = (
        lax.broadcasted_iota(jnp.int32, (plan.sy, by), 0) // BW
        == lax.broadcasted_iota(jnp.int32, (plan.sy, by), 1)
    ).astype(jnp.float32)
    means = jnp.concatenate(
        [exact(gather_y, jnp.broadcast_to(s, (plan.sy, LANES))) for s in sums], axis=0
    ) * (1.0 / (BW * BW * plan.nz))
    softplus = jnp.maximum(means, 0.0) + jnp.log(1.0 + jnp.exp(-jnp.abs(means)))
    rank_x, rank_y = lax.axis_index("gx"), lax.axis_index("gy")
    box = lax.broadcasted_iota(jnp.int32, (boxes, plan.slots), 0)
    slot = lax.broadcasted_iota(jnp.int32, (boxes, plan.slots), 1)
    device, local = quotient(destination[...], boxes)
    device_x, device_y = quotient(device, plan.gy)
    local_x, local_y = quotient(local, by)
    source_x, source_y = quotient(box, by)
    offset_x = (device_x - rank_x) * bx + local_x - source_x + (1 + bx * plan.gx)
    offset_y = (device_y - rank_y) * by + local_y - source_y + (1 + by * plan.gy)
    offset_x = quotient(offset_x, bx * plan.gx)[1]
    offset_y = quotient(offset_y, by * plan.gy)[1]
    code = (offset_x * 3 + offset_y).astype(jnp.float32)
    line = lax.broadcasted_iota(jnp.int32, (boxes, boxes), 0)
    used = jnp.where(
        line == lax.broadcasted_iota(jnp.int32, (boxes, boxes), 1), counts[...], 0
    )
    used = jnp.sum(used, axis=1, keepdims=True)
    live = jnp.where(slot < used, multiplicity[...], 0.0)
    half = plan.slots // 2
    order = pairing[...]
    index = jnp.concatenate([order, order[:, half:], order[:, :half]], axis=1)

    def gather(value):
        twice = jnp.concatenate([value, value], axis=1)
        return jnp.take_along_axis(twice, index, axis=1, mode="promise_in_bounds")

    radius_sq, live, code = gather(radius[...]), gather(live), gather(code)
    grown_sq = radius_sq + GROWTH * softplus
    root = jnp.sqrt(grown_sq)
    mass = grown_sq * root
    lane = lax.broadcasted_iota(jnp.int32, (boxes, LANES), 1)
    own = lane < plan.slots
    condensed = jnp.sum(
        jnp.where(own, live * (mass - radius_sq * jnp.sqrt(radius_sq)), 0.0),
        axis=1, keepdims=True,
    )
    condensed = jnp.broadcast_to(condensed, (boxes, LANES))
    for big in range(bx):
        less = CONDENSE * exact(spread_y, condensed[big * by : (big + 1) * by])
        for x in range(big * BW, (big + 1) * BW):
            vapour_new[x] = moist[x] - less

    def partner(value):
        return pltpu.roll(value, LANES - plan.slots, 1)

    other_grown, other_root, other_mass = partner(grown_sq), partner(root), partner(mass)
    both = root + other_root
    rate = both * both * jnp.abs(grown_sq - other_grown) * partner(live)
    final = (mass + COLLISION * rate * other_mass) / (1.0 + COLLISION * rate)
    weight = jnp.where(own, live, 0.0)
    loads = (weight, weight * final, weight * final * final)
    parts = [[], [], []]
    for direction in range(9):
        chosen = code == float(direction)
        for k in range(3):
            parts[k].append(
                jnp.sum(jnp.where(chosen, loads[k], 0.0), axis=1, keepdims=True)
            )
    payload = jnp.zeros((1, LANES), jnp.float32)
    stays = jnp.zeros((8, LANES), jnp.float32)
    line = lax.broadcasted_iota(jnp.int32, (8, LANES), 0)
    lane = lax.broadcasted_iota(jnp.int32, (1, LANES), 1)
    width = payload_width(plan)
    leaving = (lane >= boxes) & (lane < boxes + width)
    for k in range(3):
        column = jnp.concatenate(parts[k], axis=0)
        landed = jnp.sum(column * goes[...], axis=0, keepdims=True)
        stays = jnp.where(line == k, landed, stays)
        payload = payload + pltpu.roll(
            jnp.where(leaving, landed, 0.0), (k * width - boxes) % LANES, 1
        )
    stay[...] = stays
    owner = jnp.full((1, LANES), -1, jnp.int32)
    for k, (sx, sy) in enumerate(KINDS):
        to_x = lax.rem(rank_x + (sx + plan.gx), plan.gx)
        to_y = lax.rem(rank_y + (sy + plan.gy), plan.gy)
        owner = jnp.where(kind[...] == k, to_x * plan.gy + to_y, owner)
    every = lax.broadcasted_iota(jnp.int32, (plan.nd, LANES), 0)
    leave[...] = jnp.where(every == owner, payload, 0.0)


def call(body, outs, args, flops, scratch=(), space=VMEM, limit=8 * 2**20):
    moved = sum(a.size * a.dtype.itemsize for a in args)
    moved += sum(math.prod(o) * 4 for o in outs)
    return pl.pallas_call(
        body,
        out_shape=[jax.ShapeDtypeStruct(o, jnp.float32) for o in outs],
        in_specs=[space] * len(args),
        out_specs=[VMEM] * len(outs),
        scratch_shapes=list(scratch),
        compiler_params=pltpu.CompilerParams(vmem_limit_bytes=limit),
        cost_estimate=pl.CostEstimate(flops=flops, bytes_accessed=moved, transcendentals=0),
    )(*args)


def swap(block, axis):
    first, second = neighbours(lax.axis_size(axis))
    return (lambda a, b: (lax.ppermute(a, axis, first), lax.ppermute(b, axis, second)))(*block)


def exchange(chunks, plan, rows):
    flat = chunks.reshape(plan.nd, 1, rows * LANES)
    flat = lax.all_to_all(flat, ("gx", "gy"), split_axis=0, concat_axis=0, tiled=True)
    return flat.reshape(plan.nd * rows, LANES)


def shards(velocity, theta, vapour, radius_sq, multiplicity, counts, pairing, destination):
    span_x, span_y, levels = theta.shape
    slots = radius_sq.shape[0]
    plan = Plan(lax.axis_size("gx"), lax.axis_size("gy"), span_x, span_y, levels, slots)
    rank_x, rank_y = lax.axis_index("gx"), lax.axis_index("gy")
    rank = rank_x * plan.gy + rank_y
    forward, backward, q1, qy, ex, ey, ez = plan.tables()
    goes, place, kind = droplet_tables(plan)
    block = (span_x, span_y, levels)
    cells = math.prod(block)

    plane, rows = (5, span_y, levels), (5, span_x, levels)
    fields = (velocity, theta, vapour)
    (xb,) = call(
        functools.partial(far_kernel, plan), (plane,), fields, cells,
        [pltpu.SemaphoreType.DMA((3,))], HBM, EDGE_LIMIT,
    )
    xa, ya, yb = call(
        functools.partial(near_kernel, plan), (plane, rows, rows), fields + (xb,), cells,
        [pltpu.VMEM((5, span_x, 8, levels), jnp.float32)] * 2 + [pltpu.SemaphoreType.DMA((3, 3))],
        HBM, EDGE_LIMIT,
    )
    xa, xb = swap((xa, xb), "gx")
    ya, yb = swap((ya, yb), "gy")

    star, chunks = call(
        functools.partial(wind_kernel, plan),
        ((3,) + block, (plan.nd * plan.rows1, LANES)),
        (velocity, theta, xa, xb, ya, yb) + halves(forward),
        100 * cells,
    )
    spectral = exchange(chunks, plan, plan.rows1)

    theta_new, vapour_new, stay, leave = call(
        functools.partial(scalar_kernel, plan),
        (block, block, (8, LANES), (plan.nd, LANES)),
        fields + (xa, xb, ya, yb, radius_sq.T, multiplicity.T, counts[None], pairing)
        + (destination.T, goes, kind),
        100 * cells,
        (pltpu.VMEM(block, jnp.float32),),
    )

    modes = lax.dynamic_slice(jnp.asarray(ez, jnp.float32), (rank * plan.per,), (plan.per,))
    eigen = (
        jnp.asarray(ex, jnp.float32)[:, None, None]
        + jnp.asarray(ey, jnp.float32)[None, None, :]
        + modes[None, :, None]
    ).reshape(plan.tx, plan.per * plan.ty)
    inverse = jnp.where(eigen == 0.0, 0.0, 1.0 / jnp.where(eigen == 0.0, 1.0, eigen))
    (chunks,) = call(
        functools.partial(solve_kernel, plan),
        ((plan.nd * plan.rows2, LANES),),
        (spectral, inverse, leave, np.stack(halves(qy)), np.stack(halves(q1) + halves(q1.T))),
        1000 * cells,
        [pltpu.VMEM((2, plan.gy * LANES, plan.x4 * plan.ty), jnp.bfloat16)],
    )
    modal = exchange(chunks, plan, plan.rows2)

    velocity_new, moments = call(
        functools.partial(project_kernel, plan),
        ((3,) + block, (3, plan.boxes)),
        (modal, star, stay) + halves(backward) + (place,),
        100 * cells,
        (pltpu.VMEM((LANES, levels), jnp.float32),),
    )
    return (velocity_new, theta_new, vapour_new, moments)


def solution(mesh):
    placed = (
        P(None, "gx", "gy", None),
        P("gx", "gy", None),
        P("gx", "gy", None),
        P(None, ("gx", "gy")),
        P(None, ("gx", "gy")),
        P(("gx", "gy")),
        P(("gx", "gy"), None),
        P(None, ("gx", "gy")),
    )
    return jax.shard_map(
        shards,
        mesh=mesh,
        in_specs=placed,
        out_specs=(
            P(None, "gx", "gy", None),
            P("gx", "gy", None),
            P("gx", "gy", None),
            P(None, ("gx", "gy")),
        ),
        check_vma=False,
    )
```

```python
import functools
import math

import jax
import jax.numpy as jnp
import ml_dtypes
import numpy as np
from jax import lax
from jax.experimental import pallas as pl
from jax.experimental.pallas import tpu as pltpu
from jax.sharding import PartitionSpec as P

BW = 4
LANES = 128

TIME_STEP = 0.2
DIFFUSION = 0.05
BUOYANCY = 0.5
GROWTH = 0.5
COLLISION = 0.05
CONDENSE = 0.002

VMEM = pl.BlockSpec(memory_space=pltpu.VMEM)
HBM = pl.BlockSpec(memory_space=pltpu.HBM)
NT = (((1,), (1,)), ((), ()))
TN = (((0,), (0,)), ((), ()))
NN = (((1,), (0,)), ((), ()))

KINDS = [(sx, sy) for sx in (-1, 0, 1) for sy in (-1, 0, 1) if (sx, sy) != (0, 0)]


def halves(table):
    high = table.astype(np.float32).astype(ml_dtypes.bfloat16)
    low = (table - high.astype(np.float64)).astype(np.float32).astype(ml_dtypes.bfloat16)
    return high, low


def on_left(table):
    high, low = halves(table)
    return np.block([[high, high], [low, np.zeros_like(low)]])


def on_right(table):
    high, low = halves(table)
    return np.block([[high, low], [high, np.zeros_like(low)]])


def split(value, axis):
    high = value.astype(jnp.bfloat16)
    low = (value - high.astype(jnp.float32)).astype(jnp.bfloat16)
    return jnp.concatenate([high, low], axis=axis)


def from_left(table, value, turned=False):
    out = lax.dot_general(
        table, split(value, 1 if turned else 0), NT if turned else NN,
        preferred_element_type=jnp.float32,
    )
    rows = out.shape[0] // 2
    return out[:rows] + out[rows:]


def from_right(value, table, turned=False):
    out = lax.dot_general(
        split(value, 0 if turned else 1), table, TN if turned else NN,
        preferred_element_type=jnp.float32,
    )
    columns = out.shape[1] // 2
    return out[:, :columns] + out[:, columns:]


def real_basis(length):
    position = np.arange(length)[:, None]
    column = np.arange(length)
    wave = np.where(column <= length // 2, column, column - length // 2)
    angle = 2.0 * np.pi * ((position * wave[None, :]) % length) / length
    table = np.where(column[None, :] <= length // 2, np.cos(angle), np.sin(angle))
    table = table * np.sqrt(2.0 / length)
    table[:, 0] *= np.sqrt(0.5)
    if length % 2 == 0:
        table[:, length // 2] *= np.sqrt(0.5)
    return table, -4.0 * np.sin(np.pi * wave / length) ** 2


class Plan:
    def __init__(self, grid_x, grid_y, span_x, span_y, levels, slots):
        self.gx, self.gy = grid_x, grid_y
        self.sx, self.sy, self.nz = span_x, span_y, levels
        self.nd = grid_x * grid_y
        self.per = levels // self.nd
        self.x4 = LANES // span_y
        self.xg = span_x // self.x4
        self.main = self.per * self.xg
        self.rows1 = self.main + 2
        self.rows2 = self.main + 3
        self.tx, self.ty = grid_x * span_x, grid_y * span_y
        self.bx, self.by = span_x // BW, span_y // BW
        self.boxes = self.bx * self.by
        self.slots = slots

    def tables(self):
        nd, per, nz = self.nd, self.per, self.nz
        z = np.arange(nz)
        cosine = np.cos(np.pi / nz * (((2 * z[:, None] + 1) * z[None, :]) % (4 * nz)) / 2.0)
        mode = (np.arange(nd)[None, :] * per + np.arange(per)[:, None]).reshape(-1)
        forward = cosine.T[mode]
        weight = np.where(np.arange(nz) == 0, 1.0, 2.0) / nz
        backward = forward * weight[mode][:, None]
        qx, ex = real_basis(self.tx)
        qy, ey = real_basis(self.ty)
        q1 = qx.reshape(self.gx, self.xg, self.x4, self.tx)
        q1 = q1.transpose(3, 2, 1, 0).reshape(self.tx, self.tx)
        ez = -4.0 * np.sin(np.pi * z / (2 * nz)) ** 2
        return forward, backward, q1, qy, ex, ey, ez


def neighbours(count):
    first = [(i, i ^ 1) for i in range(count)]
    second = [(i, (i + 1) % count if i % 2 else (i - 1) % count) for i in range(count)]
    return first, second


def copy_all(copies):
    for copy in copies:
        copy.start()
    for copy in copies:
        copy.wait()


def planes_kernel(plan, vel, theta, vapour, xb, xa, sems):
    odd = lax.axis_index("gx") % 2
    copies = []
    for side, (out, x) in enumerate(((xb, odd), (xa, 1 - odd))):
        x = x * (plan.sx - 1)
        copies += [
            pltpu.make_async_copy(vel.at[:, x], out.at[0:3], sems.at[side, 0]),
            pltpu.make_async_copy(theta.at[x], out.at[3], sems.at[side, 1]),
            pltpu.make_async_copy(vapour.at[x], out.at[4], sems.at[side, 2]),
        ]
    for copy in copies:
        copy.start()
    for copy in copies:
        copy.wait()


def rows_kernel(plan, vel, theta, vapour, after, yb, ya):
    odd = lax.axis_index("gy") % 2 == 1
    for f, ref in enumerate((vel.at[0], vel.at[1], vel.at[2], theta, vapour)):
        for x in range(plan.sx):
            low, high = ref[x, 0:1], ref[x, plan.sy - 1 :]
            ya[f, x : x + 1] = jnp.where(odd, low, high)
            yb[f, x : x + 1] = jnp.where(odd, high, low)


def edge_masks(plan):
    row = lax.broadcasted_iota(jnp.int32, (plan.sy, plan.nz), 0)
    lane = lax.broadcasted_iota(jnp.int32, (plan.sy, plan.nz), 1)
    return row == 0, row == plan.sy - 1, lane == 0, lane == plan.nz - 1


def coefficients(u, v, w):
    half = 0.5 * TIME_STEP
    side = TIME_STEP * DIFFUSION
    return (
        side - half * u, side + half * u,
        side - half * v, side + half * v,
        side - half * w, side + half * w,
    )


def advect(c, east, west, north_row, south_row, coef, masks, plan):
    row0, row_last, lane0, lane_last = masks
    north = jnp.where(row_last, north_row, pltpu.roll(c, plan.sy - 1, 0))
    south = jnp.where(row0, south_row, pltpu.roll(c, 1, 0))
    upper = jnp.where(lane_last, c, pltpu.roll(c, plan.nz - 1, 1))
    lower = jnp.where(lane0, c, pltpu.roll(c, 1, 1))
    ce, cw, cn, cs, cu, cl = coef
    return (
        (1.0 - 6.0 * TIME_STEP * DIFFUSION) * c
        + (ce * east + cw * west)
        + (cn * north + cs * south)
        + (cu * upper + cl * lower)
    )


def side_planes(xa, xb, f):
    odd = lax.axis_index("gx") % 2 == 1
    return jnp.where(odd, xa[f], xb[f]), jnp.where(odd, xb[f], xa[f])


def side_rows(ya, yb, f):
    odd = lax.axis_index("gy") % 2 == 1
    return jnp.where(odd, ya[f], yb[f]), jnp.where(odd, yb[f], ya[f])


def before(value, axis):
    at = lax.broadcasted_iota(jnp.int32, value.shape, axis)
    return jnp.where(at == 0, 0.0, pltpu.roll(value, 1, axis))


def inner_kernel(plan, vel, theta, div, along_x, along_y):
    masks = edge_masks(plan)
    zero = jnp.zeros((plan.sy, plan.nz), jnp.float32)
    zero_row = jnp.zeros((1, plan.nz), jnp.float32)
    last = plan.sx - 1
    last_u = None
    for x in range(plan.sx):
        coef = coefficients(vel[0, x], vel[1, x], vel[2, x])
        u, v, w = (
            advect(
                vel[f, x],
                vel[f, x + 1] if x < last else zero,
                vel[f, x - 1] if x else zero,
                zero_row, zero_row, coef, masks, plan,
            )
            for f in range(3)
        )
        w = w + (TIME_STEP * BUOYANCY) * theta[x]
        total = (u if last_u is None else u - last_u) + (v - before(v, 0)) + (w - before(w, 1))
        div[x] = total
        last_u = u
        along_y[0, x : x + 1] = v[plan.sy - 1 : plan.sy]
        along_y[1, x : x + 1] = coef[3][0:1]
        along_y[2, x : x + 1] = coef[2][plan.sy - 1 : plan.sy]
        if x == 0:
            along_x[1] = coef[1]
        if x == last:
            along_x[0] = u
            along_x[2] = coef[0]


def spread_kernel(plan, div, along_x, along_y, xb, yb, xa, ya, forward, out):
    sides = [side_planes(xa, xb, f) for f in range(3)]
    ends = [side_rows(ya, yb, f) for f in range(3)]
    west_u, west_v, west_w = (along_x[1] * west for west, _ in sides)
    east_u, east_v, east_w = (along_x[2] * east for _, east in sides)
    south_u, south_v, south_w = (along_y[1] * south for south, _ in ends)
    north_u, north_v, north_w = (along_y[2] * north for _, north in ends)
    first_row = south_u - before(south_u, 0) + south_v + south_w - before(south_w, 1)
    last_row = north_u - before(north_u, 0) + north_v + north_w - before(north_w, 1)
    row = lax.broadcasted_iota(jnp.int32, (plan.sy, plan.nz), 0)
    last = plan.sx - 1
    slab = []
    for x in range(plan.sx):
        at = slice(x, x + 1)
        total = div[x] + jnp.where(
            row == 0,
            first_row[at],
            jnp.where(
                row == 1, -south_v[at], jnp.where(row == plan.sy - 1, last_row[at], 0.0)
            ),
        )
        if x == 0:
            total = total + west_u + (west_v - before(west_v, 0)) + (west_w - before(west_w, 1))
        if x == 1:
            total = total - west_u
        if x == last:
            total = total + east_u + (east_v - before(east_v, 0)) + (east_w - before(east_w, 1))
        slab.append(total)
    last_u = along_x[0] + east_u + jnp.where(
        row == 0, south_u[last:], jnp.where(row == plan.sy - 1, north_u[last:], 0.0)
    )
    column = lax.broadcasted_iota(jnp.int32, (plan.sx, plan.nz), 0)
    last_v = along_y[0] + north_v + jnp.where(
        column == 0,
        west_v[plan.sy - 1 :],
        jnp.where(column == last, east_v[plan.sy - 1 :], 0.0),
    )
    tiled_plane = jnp.concatenate([-last_u] * plan.x4, axis=0)
    tiled_rows = []
    for p in range(plan.x4):
        block = jnp.zeros((plan.sy, plan.nz), jnp.float32)
        for g in range(plan.xg):
            at = g * plan.x4 + p
            block = jnp.where(row % plan.xg == g, -last_v[at : at + 1], block)
        tiled_rows.append(block)
    modes = from_left(
        forward[...], jnp.concatenate(slab + [tiled_plane] + tiled_rows, axis=0), turned=True
    )
    for g in range(plan.xg):
        for j in range(plan.per):
            out[pl.ds(j * plan.xg + g, plan.nd, stride=plan.rows1), :] = modes[
                j * plan.nd : (j + 1) * plan.nd, g * LANES : (g + 1) * LANES
            ]
    extra = modes[:, plan.xg * LANES :]
    lane = lax.broadcasted_iota(jnp.int32, (plan.nd, LANES), 1)
    plane_sum = jnp.zeros((plan.nd, LANES), jnp.float32)
    row_sum = jnp.zeros((plan.nd, LANES), jnp.float32)
    for j in range(plan.per):
        part = extra[j * plan.nd : (j + 1) * plan.nd]
        plane_sum = jnp.where(lane // plan.sy == j, part[:, :LANES], plane_sum)
        row_sum = jnp.where(lane % plan.sy // plan.xg == j, part[:, LANES:], row_sum)
    out[pl.ds(plan.main, plan.nd, stride=plan.rows1), :] = plane_sum
    out[pl.ds(plan.main + 1, plan.nd, stride=plan.rows1), :] = row_sum


def regroup(parts, plan):
    group = lax.broadcasted_iota(jnp.int32, parts[0].shape, 1) // plan.sy
    parts = list(parts)
    distance = plan.x4 // 2
    while distance:
        lower = group & distance == 0
        step = distance * plan.sy
        for i in range(plan.x4):
            if not i & distance:
                one, two = parts[i], parts[i + distance]
                parts[i] = jnp.where(lower, one, pltpu.roll(two, step, 1))
                parts[i + distance] = jnp.where(lower, pltpu.roll(one, LANES - step, 1), two)
        distance //= 2
    return parts


def solve_kernel(plan, r, leave, eigen_x, eigen_yz, tables, out):
    wide_x, wide_y = 2 * plan.tx, 2 * plan.ty
    fy, by = tables[0, :wide_y, :wide_y], tables[1, :wide_y, :wide_y]
    fx, bx = tables[2, :wide_x, :wide_x], tables[3, :wide_x, :wide_x]
    rank = lax.axis_index("gx") * plan.gy + lax.axis_index("gy")
    eigen = eigen_x[...] + eigen_yz[pl.ds(rank, 1), :]
    inverse = jnp.where(eigen == 0.0, 0.0, 1.0 / jnp.where(eigen == 0.0, 1.0, eigen))
    gx, gy, per, xg, x4 = plan.gx, plan.gy, plan.per, plan.xg, plan.x4
    lane = lax.broadcasted_iota(jnp.int32, (gx, LANES), 1)
    first_lanes = lane < plan.sy
    first_rows = lane % plan.sy == 0
    step1, step2 = gy * plan.rows1, gy * plan.rows2

    def take(b, q):
        return r[pl.ds(b * plan.rows1 + q, gx, stride=step1), :]

    blocks = [[take(b, q) for q in range(plan.main)] for b in range(gy)]
    for b in range(gy):
        plane = pltpu.roll(take(b, plan.main), 1, 0)
        for j in range(per):
            moved = plane if j == 0 else pltpu.roll(plane, LANES - j * plan.sy, 1)
            blocks[b][j * xg] = blocks[b][j * xg] + jnp.where(first_lanes, moved, 0.0)
        rows = take(b, plan.main + 1)
        for q in range(plan.main):
            moved = rows if q == 0 else pltpu.roll(rows, LANES - q, 1)
            nb = (b + 1) % gy
            blocks[nb][q] = blocks[nb][q] + jnp.where(first_rows, moved, 0.0)
    turned = [
        [regroup([blocks[h + i][q] for i in range(x4)], plan) for h in range(0, gy, x4)]
        for q in range(plan.main)
    ]
    grid = jnp.concatenate(
        [
            jnp.concatenate([part[p] for part in turned[q]], axis=1)
            for p in range(x4)
            for q in range(plan.main)
        ],
        axis=0,
    )
    in_y = from_right(grid, fy)
    height = xg * gx

    def piece(value, row, column):
        return value[row * height : (row + 1) * height, column * plan.ty : (column + 1) * plan.ty]

    in_y = jnp.concatenate(
        [
            jnp.concatenate([piece(in_y, p * per + j, 0) for p in range(x4)], axis=0)
            for j in range(per)
        ],
        axis=1,
    )
    solved = from_left(fx, in_y) * inverse
    in_x = from_left(bx, solved)
    in_x = jnp.concatenate([piece(in_x, p, j) for p in range(x4) for j in range(per)], axis=0)
    grid = from_right(in_x, by)
    blocks = [[None] * plan.main for _ in range(gy)]
    for q in range(plan.main):
        for h in range(0, gy, x4):
            parts = [
                grid[
                    (p * plan.main + q) * gx : (p * plan.main + q + 1) * gx,
                    h * plan.sy : h * plan.sy + LANES,
                ]
                for p in range(x4)
            ]
            for i, part in enumerate(regroup(parts, plan)):
                blocks[h + i][q] = part
    planes = [jnp.zeros((gx, LANES), jnp.float32) for _ in range(gy)]
    rows = [jnp.zeros((gx, LANES), jnp.float32) for _ in range(gy)]
    for b in range(gy):
        for q in range(plan.main):
            block = blocks[b][q]
            out[pl.ds(b * plan.rows2 + q, gx, stride=step2), :] = block
            moved = jnp.where(first_rows, block, 0.0)
            nb = (b - 1) % gy
            rows[nb] = rows[nb] + (moved if q == 0 else pltpu.roll(moved, q, 1))
            if q % xg == 0:
                j = q // xg
                moved = jnp.where(first_lanes, block, 0.0)
                planes[b] = planes[b] + (moved if j == 0 else pltpu.roll(moved, j * plan.sy, 1))
    for b in range(gy):
        out[pl.ds(b * plan.rows2 + plan.main, gx, stride=step2), :] = pltpu.roll(
            planes[b], gx - 1, 0
        )
        out[pl.ds(b * plan.rows2 + plan.main + 1, gx, stride=step2), :] = rows[b]
    out[pl.ds(plan.main + 2, plan.nd, stride=plan.rows2), :] = leave[...]


def project_kernel(plan, r, star, stay, backward, place, vel_new, moments, scratch):
    nd, per, xg, x4, sy, sx = plan.nd, plan.per, plan.xg, plan.x4, plan.sy, plan.sx
    lane = lax.broadcasted_iota(jnp.int32, (nd, LANES), 1)

    def take(q):
        return r[pl.ds(q, nd, stride=plan.rows2), :]

    planes, rows = take(plan.main), take(plan.main + 1)
    wide = jnp.concatenate(
        [
            jnp.concatenate([jnp.where(lane // sy == j, planes, 0.0) for j in range(per)], axis=0),
            jnp.concatenate(
                [jnp.where(lane % sy // xg == j, rows, 0.0) for j in range(per)], axis=0
            ),
        ],
        axis=1,
    )
    modes = [
        jnp.concatenate([take(j * xg + g) for j in range(per)], axis=0) for g in range(xg)
    ]
    cells = from_right(jnp.concatenate(modes + [wide], axis=1), backward[...], turned=True)
    extra = cells[xg * LANES :]
    beyond = extra[0:sy]
    for j in range(1, per):
        beyond = beyond + extra[j * sy : (j + 1) * sy]
    scratch[...] = extra[LANES:]
    row = lax.broadcasted_iota(jnp.int32, (sy, plan.nz), 0)
    level = lax.broadcasted_iota(jnp.int32, (sy, plan.nz), 1)
    pressure = [cells[x * sy : (x + 1) * sy] for x in range(sx)]
    pressure.append(beyond)
    for x in range(sx):
        here = pressure[x]
        g, p = x // x4, x % x4
        last = scratch[p * sy + g : p * sy + g + 1]
        for j in range(1, per):
            last = last + scratch[p * sy + j * xg + g : p * sy + j * xg + g + 1]
        north = jnp.where(row == sy - 1, last, pltpu.roll(here, sy - 1, 0))
        upper = jnp.where(level == plan.nz - 1, here, pltpu.roll(here, plan.nz - 1, 1))
        vel_new[0, x] = star[0, x] - (pressure[x + 1] - here)
        vel_new[1, x] = star[1, x] - (north - here)
        vel_new[2, x] = star[2, x] - (upper - here)
    came = jnp.sum(take(plan.main + 2), axis=0, keepdims=True)
    load = lax.broadcasted_iota(jnp.int32, (8, LANES), 0)
    at = lax.broadcasted_iota(jnp.int32, (8, LANES), 1)
    width = payload_width(plan)
    loads = jnp.where(at // width == load, came, 0.0)
    total = stay[...] + lax.dot_general(
        loads, place[...], NN, precision=lax.Precision.HIGHEST, preferred_element_type=jnp.float32
    )
    moments[...] = total[:3, : plan.boxes] * (1.0 / plan.slots)


def payload_width(plan):
    return 2 * plan.by + 2 * plan.bx + 4


def droplet_tables(plan):
    bx, by, boxes = plan.bx, plan.by, plan.boxes
    width = payload_width(plan)
    lane_of = {}
    kind_of = np.full((LANES,), -1)
    place = np.zeros((LANES, LANES), np.float32)
    for k, (sx, sy) in enumerate(KINDS):
        xs = range(bx) if sx == 0 else [0 if sx > 0 else bx - 1]
        ys = range(by) if sy == 0 else [0 if sy > 0 else by - 1]
        for x in xs:
            for y in ys:
                lane_of[k, x, y] = len(lane_of)
    assert len(lane_of) == width and max(3 * width, boxes + width) <= LANES
    for (k, x, y), at in lane_of.items():
        for load in range(3):
            kind_of[load * width + at] = k
            place[load * width + at, x * by + y] = 1.0
    goes = np.zeros((9 * boxes, LANES), np.float32)
    for dx in (-1, 0, 1):
        for dy in (-1, 0, 1):
            code = (dx + 1) * 3 + dy + 1
            for x in range(bx):
                for y in range(by):
                    line = code * boxes + x * by + y
                    sx = (x + dx) // bx
                    sy = (y + dy) // by
                    tx, ty = (x + dx) % bx, (y + dy) % by
                    if (sx, sy) == (0, 0):
                        goes[line, tx * by + ty] = 1.0
                    else:
                        goes[line, boxes + lane_of[KINDS.index((sx, sy)), tx, ty]] = 1.0
    return goes, place, kind_of[None].astype(np.int32)


def quotient(value, divisor):
    if divisor & (divisor - 1) == 0:
        return value >> (divisor.bit_length() - 1), value & (divisor - 1)
    return lax.div(value, divisor), lax.rem(value, divisor)


def scalar_kernel(
    plan, vel, theta, vapour, xb, yb, xa, ya, radius, multiplicity, counts, pairing,
    destination, goes, kind, star, theta_new, vapour_new, stay, leave, moist,
):
    masks = edge_masks(plan)
    bx, by, boxes = plan.bx, plan.by, plan.boxes
    edges = []
    for f in range(5):
        west, east = side_planes(xa, xb, f)
        south, north = side_rows(ya, yb, f)
        edges.append((west, east, south, north))
    sums = []
    total = None
    for x in range(plan.sx):
        coef = coefficients(vel[0, x], vel[1, x], vel[2, x])
        for f, (west, east, south, north) in enumerate(edges):
            ref = (vel.at[0], vel.at[1], vel.at[2], theta, vapour)[f]
            new = (star.at[0], star.at[1], star.at[2], theta_new, moist)[f]
            moved = advect(
                ref[x],
                ref[x + 1] if x < plan.sx - 1 else east,
                ref[x - 1] if x else west,
                north[x : x + 1], south[x : x + 1], coef, masks, plan,
            )
            if f == 2:
                moved = moved + (TIME_STEP * BUOYANCY) * theta[x]
            new[x] = moved
        total = moved if x % BW == 0 else total + moved
        if x % BW == BW - 1:
            sums.append(jnp.sum(total, axis=1, keepdims=True))
    exact = functools.partial(
        lax.dot_general, dimension_numbers=NN, precision=lax.Precision.HIGHEST,
        preferred_element_type=jnp.float32,
    )
    gather_y = (
        lax.broadcasted_iota(jnp.int32, (by, plan.sy), 1) // BW
        == lax.broadcasted_iota(jnp.int32, (by, plan.sy), 0)
    ).astype(jnp.float32)
    spread_y = (
        lax.broadcasted_iota(jnp.int32, (plan.sy, by), 0) // BW
        == lax.broadcasted_iota(jnp.int32, (plan.sy, by), 1)
    ).astype(jnp.float32)
    means = jnp.concatenate(
        [exact(gather_y, jnp.broadcast_to(s, (plan.sy, LANES))) for s in sums], axis=0
    ) * (1.0 / (BW * BW * plan.nz))
    softplus = jnp.maximum(means, 0.0) + jnp.log(1.0 + jnp.exp(-jnp.abs(means)))
    rank_x, rank_y = lax.axis_index("gx"), lax.axis_index("gy")
    box = lax.broadcasted_iota(jnp.int32, (boxes, plan.slots), 0)
    slot = lax.broadcasted_iota(jnp.int32, (boxes, plan.slots), 1)
    device, local = quotient(destination[...], boxes)
    device_x, device_y = quotient(device, plan.gy)
    local_x, local_y = quotient(local, by)
    source_x, source_y = quotient(box, by)
    offset_x = (device_x - rank_x) * bx + local_x - source_x + (1 + bx * plan.gx)
    offset_y = (device_y - rank_y) * by + local_y - source_y + (1 + by * plan.gy)
    offset_x = quotient(offset_x, bx * plan.gx)[1]
    offset_y = quotient(offset_y, by * plan.gy)[1]
    code = (offset_x * 3 + offset_y).astype(jnp.float32)
    line = lax.broadcasted_iota(jnp.int32, (boxes, boxes), 0)
    used = jnp.where(
        line == lax.broadcasted_iota(jnp.int32, (boxes, boxes), 1), counts[...], 0
    )
    used = jnp.sum(used, axis=1, keepdims=True)
    live = jnp.where(slot < used, multiplicity[...], 0.0)
    half = plan.slots // 2
    order = pairing[...]
    index = jnp.concatenate([order, order[:, half:], order[:, :half]], axis=1)

    def gather(value):
        twice = jnp.concatenate([value, value], axis=1)
        return jnp.take_along_axis(twice, index, axis=1, mode="promise_in_bounds")

    radius_sq, live, code = gather(radius[...]), gather(live), gather(code)
    grown_sq = radius_sq + GROWTH * softplus
    root = jnp.sqrt(grown_sq)
    mass = grown_sq * root
    lane = lax.broadcasted_iota(jnp.int32, (boxes, LANES), 1)
    own = lane < plan.slots
    condensed = jnp.sum(
        jnp.where(own, live * (mass - radius_sq * jnp.sqrt(radius_sq)), 0.0),
        axis=1, keepdims=True,
    )
    condensed = jnp.broadcast_to(condensed, (boxes, LANES))
    for big in range(bx):
        less = CONDENSE * exact(spread_y, condensed[big * by : (big + 1) * by])
        for x in range(big * BW, (big + 1) * BW):
            vapour_new[x] = moist[x] - less

    def partner(value):
        return pltpu.roll(value, LANES - plan.slots, 1)

    other_grown, other_root, other_mass = partner(grown_sq), partner(root), partner(mass)
    both = root + other_root
    rate = both * both * jnp.abs(grown_sq - other_grown) * partner(live)
    final = (mass + COLLISION * rate * other_mass) / (1.0 + COLLISION * rate)
    weight = jnp.where(own, live, 0.0)
    loads = (weight, weight * final, weight * final * final)
    parts = [[], [], []]
    for direction in range(9):
        chosen = code == float(direction)
        for k in range(3):
            parts[k].append(
                jnp.sum(jnp.where(chosen, loads[k], 0.0), axis=1, keepdims=True)
            )
    payload = jnp.zeros((1, LANES), jnp.float32)
    stays = jnp.zeros((8, LANES), jnp.float32)
    line = lax.broadcasted_iota(jnp.int32, (8, LANES), 0)
    lane = lax.broadcasted_iota(jnp.int32, (1, LANES), 1)
    width = payload_width(plan)
    leaving = (lane >= boxes) & (lane < boxes + width)
    for k in range(3):
        column = jnp.concatenate(parts[k], axis=0)
        landed = jnp.sum(column * goes[...], axis=0, keepdims=True)
        stays = jnp.where(line == k, landed, stays)
        payload = payload + pltpu.roll(
            jnp.where(leaving, landed, 0.0), (k * width - boxes) % LANES, 1
        )
    stay[...] = stays
    owner = jnp.full((1, LANES), -1, jnp.int32)
    for k, (sx, sy) in enumerate(KINDS):
        to_x = lax.rem(rank_x + (sx + plan.gx), plan.gx)
        to_y = lax.rem(rank_y + (sy + plan.gy), plan.gy)
        owner = jnp.where(kind[...] == k, to_x * plan.gy + to_y, owner)
    every = lax.broadcasted_iota(jnp.int32, (plan.nd, LANES), 0)
    leave[...] = jnp.where(every == owner, payload, 0.0)


def call(body, outs, args, flops, scratch=(), space=VMEM):
    moved = sum(a.size * a.dtype.itemsize for a in args)
    moved += sum(math.prod(o) * 4 for o in outs)
    return pl.pallas_call(
        body,
        out_shape=[jax.ShapeDtypeStruct(o, jnp.float32) for o in outs],
        in_specs=[space] * len(args),
        out_specs=[VMEM] * len(outs),
        scratch_shapes=list(scratch),
        compiler_params=pltpu.CompilerParams(vmem_limit_bytes=16 * 2**20),
        cost_estimate=pl.CostEstimate(flops=flops, bytes_accessed=moved, transcendentals=0),
    )(*args)


def exchange(chunks, plan, rows):
    flat = chunks.reshape(plan.nd, 1, rows * LANES)
    flat = lax.all_to_all(flat, ("gx", "gy"), split_axis=0, concat_axis=0, tiled=True)
    return flat.reshape(plan.nd * rows, LANES)


def shards(velocity, theta, vapour, radius_sq, multiplicity, counts, pairing, destination):
    span_x, span_y, levels = theta.shape
    slots = radius_sq.shape[0]
    plan = Plan(lax.axis_size("gx"), lax.axis_size("gy"), span_x, span_y, levels, slots)
    forward, backward, q1, qy, ex, ey, ez = plan.tables()
    goes, place, kind = droplet_tables(plan)
    block = (span_x, span_y, levels)
    cells = math.prod(block)

    plane, rows = (5, span_y, levels), (5, span_x, levels)
    fields = (velocity, theta, vapour)
    placed = [pltpu.with_memory_space_constraint(f, pltpu.HBM) for f in fields]
    xb, xa = call(
        functools.partial(planes_kernel, plan), (plane, plane), placed, cells,
        [pltpu.SemaphoreType.DMA((2, 3))], HBM,
    )
    yb, ya = call(functools.partial(rows_kernel, plan), (rows, rows), (*fields, xa), cells)
    ways_x, ways_y = neighbours(plan.gx), neighbours(plan.gy)
    xb, xa = lax.ppermute(xb, "gx", ways_x[1]), lax.ppermute(xa, "gx", ways_x[0])
    yb, ya = lax.ppermute(yb, "gy", ways_y[1]), lax.ppermute(ya, "gy", ways_y[0])
    halo = (xb, yb, xa, ya)

    inner = call(
        functools.partial(inner_kernel, plan),
        (block, (3, span_y, levels), (3, span_x, levels)), (velocity, theta), 100 * cells,
    )
    (chunks,) = call(
        functools.partial(spread_kernel, plan), ((plan.nd * plan.rows1, LANES),),
        (*inner, *halo, on_left(forward)), 100 * cells,
    )
    spectral = exchange(chunks, plan, plan.rows1)

    tables = [on_right(qy), on_right(qy.T), on_left(q1), on_left(q1.T)]
    most = max(t.shape[0] for t in tables)
    tables = np.stack([np.pad(t, (0, most - t.shape[0])) for t in tables])
    eigen_x = ex.astype(np.float32)[:, None]
    eigen_yz = (ez.reshape(plan.nd, plan.per, 1) + ey).reshape(plan.nd, -1).astype(np.float32)
    star, theta_new, vapour_new, stay, leave = call(
        functools.partial(scalar_kernel, plan),
        ((3,) + block, block, block, (8, LANES), (plan.nd, LANES)),
        fields + halo + (radius_sq.T, multiplicity.T, counts[None], pairing)
        + (destination.T, goes, kind),
        100 * cells,
        (pltpu.VMEM(block, jnp.float32),),
    )

    (chunks,) = call(
        functools.partial(solve_kernel, plan),
        ((plan.nd * plan.rows2, LANES),),
        (spectral, leave, eigen_x, eigen_yz, tables),
        1000 * cells,
    )
    modal = exchange(chunks, plan, plan.rows2)

    velocity_new, moments = call(
        functools.partial(project_kernel, plan),
        ((3,) + block, (3, plan.boxes)),
        (modal, star, stay, on_right(backward), place),
        100 * cells,
        (pltpu.VMEM((LANES, levels), jnp.float32),),
    )
    return (velocity_new, theta_new, vapour_new, moments)


def solution(mesh):
    placed = (
        P(None, "gx", "gy", None),
        P("gx", "gy", None),
        P("gx", "gy", None),
        P(None, ("gx", "gy")),
        P(None, ("gx", "gy")),
        P(("gx", "gy")),
        P(("gx", "gy"), None),
        P(None, ("gx", "gy")),
    )
    return jax.shard_map(
        shards,
        mesh=mesh,
        in_specs=placed,
        out_specs=(
            P(None, "gx", "gy", None),
            P("gx", "gy", None),
            P("gx", "gy", None),
            P(None, ("gx", "gy")),
        ),
        check_vma=False,
    )
```

```python
import functools
import math

import jax
import jax.numpy as jnp
import ml_dtypes
import numpy as np
from jax import lax
from jax.experimental import pallas as pl
from jax.experimental.pallas import tpu as pltpu
from jax.sharding import PartitionSpec as P

BW = 4
LANES = 128

TIME_STEP = 0.2
DIFFUSION = 0.05
BUOYANCY = 0.5
GROWTH = 0.5
COLLISION = 0.05
CONDENSE = 0.002

VMEM = pl.BlockSpec(memory_space=pltpu.VMEM)
HBM = pl.BlockSpec(memory_space=pltpu.HBM)
NT = (((1,), (1,)), ((), ()))
TN = (((0,), (0,)), ((), ()))
NN = (((1,), (0,)), ((), ()))

KINDS = [(sx, sy) for sx in (-1, 0, 1) for sy in (-1, 0, 1) if (sx, sy) != (0, 0)]


def halves(table):
    high = table.astype(np.float32).astype(ml_dtypes.bfloat16)
    low = (table - high.astype(np.float64)).astype(np.float32).astype(ml_dtypes.bfloat16)
    return high, low


def on_left(table):
    high, low = halves(table)
    return np.block([[high, high], [low, low]])


def on_right(table):
    high, low = halves(table)
    return np.block([[high, low], [high, low]])


def split(value, axis):
    high = value.astype(jnp.bfloat16)
    low = (value - high.astype(jnp.float32)).astype(jnp.bfloat16)
    return jnp.concatenate([high, low], axis=axis)


def from_left(table, value, turned=False):
    out = lax.dot_general(
        table, split(value, 1 if turned else 0), NT if turned else NN,
        preferred_element_type=jnp.float32,
    )
    rows = out.shape[0] // 2
    return out[:rows] + out[rows:]


def from_right(value, table, turned=False):
    out = lax.dot_general(
        split(value, 0 if turned else 1), table, TN if turned else NN,
        preferred_element_type=jnp.float32,
    )
    columns = out.shape[1] // 2
    return out[:, :columns] + out[:, columns:]


def real_basis(length):
    position = np.arange(length)[:, None]
    column = np.arange(length)
    wave = np.where(column <= length // 2, column, column - length // 2)
    angle = 2.0 * np.pi * ((position * wave[None, :]) % length) / length
    table = np.where(column[None, :] <= length // 2, np.cos(angle), np.sin(angle))
    table = table * np.sqrt(2.0 / length)
    table[:, 0] *= np.sqrt(0.5)
    if length % 2 == 0:
        table[:, length // 2] *= np.sqrt(0.5)
    return table, -4.0 * np.sin(np.pi * wave / length) ** 2


class Plan:
    def __init__(self, grid_x, grid_y, span_x, span_y, levels, slots):
        self.gx, self.gy = grid_x, grid_y
        self.sx, self.sy, self.nz = span_x, span_y, levels
        self.nd = grid_x * grid_y
        self.per = levels // self.nd
        self.x4 = LANES // span_y
        self.xg = span_x // self.x4
        self.main = self.per * self.xg
        self.rows1 = self.main + 2
        self.rows2 = self.main + 1
        self.tx, self.ty = grid_x * span_x, grid_y * span_y
        self.bx, self.by = span_x // BW, span_y // BW
        self.boxes = self.bx * self.by
        self.slots = slots
        self.width = 2 * self.by + 2 * self.bx + 4
        self.edge = 3 * self.width
        assert max(self.edge + 3 * self.per + 1, self.boxes + self.width) <= LANES

    def tables(self):
        nd, per, nz = self.nd, self.per, self.nz
        z = np.arange(nz)
        cosine = np.cos(np.pi / nz * (((2 * z[:, None] + 1) * z[None, :]) % (4 * nz)) / 2.0)
        mode = (np.arange(nd)[None, :] * per + np.arange(per)[:, None]).reshape(-1)
        forward = cosine.T[mode]
        weight = np.where(np.arange(nz) == 0, 1.0, 2.0) / nz
        backward = forward * weight[mode][:, None]
        qx, ex = real_basis(self.tx)
        qy, ey = real_basis(self.ty)
        q1 = qx.reshape(self.gx, self.xg, self.x4, self.tx)
        q1 = q1.transpose(3, 2, 1, 0).reshape(self.tx, self.tx)
        ez = -4.0 * np.sin(np.pi * z / (2 * nz)) ** 2
        return forward, backward, q1, qy, ex, ey, ez


def neighbours(count):
    first = [(i, i ^ 1) for i in range(count)]
    second = [(i, (i + 1) % count if i % 2 else (i - 1) % count) for i in range(count)]
    return first, second


def copy_all(copies):
    for copy in copies:
        copy.start()
    for copy in copies:
        copy.wait()


def planes_kernel(plan, vel, theta, vapour, xb, xa, sems):
    odd = lax.axis_index("gx") % 2
    copies = []
    for side, (out, x) in enumerate(((xb, odd), (xa, 1 - odd))):
        x = x * (plan.sx - 1)
        copies += [
            pltpu.make_async_copy(vel.at[:, x], out.at[0:3], sems.at[side, 0]),
            pltpu.make_async_copy(theta.at[x], out.at[3], sems.at[side, 1]),
            pltpu.make_async_copy(vapour.at[x], out.at[4], sems.at[side, 2]),
        ]
    for copy in copies:
        copy.start()
    for copy in copies:
        copy.wait()


def rows_kernel(plan, vel, theta, vapour, after, yb, ya):
    odd = lax.axis_index("gy") % 2 == 1
    for f, ref in enumerate((vel.at[0], vel.at[1], vel.at[2], theta, vapour)):
        for x in range(plan.sx):
            low, high = ref[x, 0:1], ref[x, plan.sy - 1 :]
            ya[f, x : x + 1] = jnp.where(odd, low, high)
            yb[f, x : x + 1] = jnp.where(odd, high, low)


def edge_masks(plan):
    row = lax.broadcasted_iota(jnp.int32, (plan.sy, plan.nz), 0)
    lane = lax.broadcasted_iota(jnp.int32, (plan.sy, plan.nz), 1)
    return row == 0, row == plan.sy - 1, lane == 0, lane == plan.nz - 1


def coefficients(u, v, w):
    half = 0.5 * TIME_STEP
    side = TIME_STEP * DIFFUSION
    return (
        side - half * u, side + half * u,
        side - half * v, side + half * v,
        side - half * w, side + half * w,
    )


def advect(c, east, west, north_row, south_row, coef, masks, plan):
    row0, row_last, lane0, lane_last = masks
    north = jnp.where(row_last, north_row, pltpu.roll(c, plan.sy - 1, 0))
    south = jnp.where(row0, south_row, pltpu.roll(c, 1, 0))
    upper = jnp.where(lane_last, c, pltpu.roll(c, plan.nz - 1, 1))
    lower = jnp.where(lane0, c, pltpu.roll(c, 1, 1))
    ce, cw, cn, cs, cu, cl = coef
    return (
        (1.0 - 6.0 * TIME_STEP * DIFFUSION) * c
        + (ce * east + cw * west)
        + (cn * north + cs * south)
        + (cu * upper + cl * lower)
    )


def side_planes(xa, xb, f):
    odd = lax.axis_index("gx") % 2 == 1
    return jnp.where(odd, xa[f], xb[f]), jnp.where(odd, xb[f], xa[f])


def side_rows(ya, yb, f):
    odd = lax.axis_index("gy") % 2 == 1
    return jnp.where(odd, ya[f], yb[f]), jnp.where(odd, yb[f], ya[f])


def before(value, axis):
    at = lax.broadcasted_iota(jnp.int32, value.shape, axis)
    return jnp.where(at == 0, 0.0, pltpu.roll(value, 1, axis))


def inner_kernel(plan, vel, theta, div, along_x, along_y):
    masks = edge_masks(plan)
    zero = jnp.zeros((plan.sy, plan.nz), jnp.float32)
    zero_row = jnp.zeros((1, plan.nz), jnp.float32)
    last = plan.sx - 1
    last_u = None
    for x in range(plan.sx):
        coef = coefficients(vel[0, x], vel[1, x], vel[2, x])
        u, v, w = (
            advect(
                vel[f, x],
                vel[f, x + 1] if x < last else zero,
                vel[f, x - 1] if x else zero,
                zero_row, zero_row, coef, masks, plan,
            )
            for f in range(3)
        )
        w = w + (TIME_STEP * BUOYANCY) * theta[x]
        total = (u if last_u is None else u - last_u) + (v - before(v, 0)) + (w - before(w, 1))
        div[x] = total
        last_u = u
        along_y[0, x : x + 1] = v[plan.sy - 1 : plan.sy]
        along_y[1, x : x + 1] = coef[3][0:1]
        along_y[2, x : x + 1] = coef[2][plan.sy - 1 : plan.sy]
        if x == 0:
            along_x[1] = coef[1]
        if x == last:
            along_x[0] = u
            along_x[2] = coef[0]


def spread_kernel(plan, div, along_x, along_y, xb, yb, xa, ya, forward, out):
    sides = [side_planes(xa, xb, f) for f in range(3)]
    ends = [side_rows(ya, yb, f) for f in range(3)]
    west_u, west_v, west_w = (along_x[1] * west for west, _ in sides)
    east_u, east_v, east_w = (along_x[2] * east for _, east in sides)
    south_u, south_v, south_w = (along_y[1] * south for south, _ in ends)
    north_u, north_v, north_w = (along_y[2] * north for _, north in ends)
    first_row = south_u - before(south_u, 0) + south_v + south_w - before(south_w, 1)
    last_row = north_u - before(north_u, 0) + north_v + north_w - before(north_w, 1)
    row = lax.broadcasted_iota(jnp.int32, (plan.sy, plan.nz), 0)
    last = plan.sx - 1
    slab = []
    for x in range(plan.sx):
        at = slice(x, x + 1)
        total = div[x] + jnp.where(
            row == 0,
            first_row[at],
            jnp.where(
                row == 1, -south_v[at], jnp.where(row == plan.sy - 1, last_row[at], 0.0)
            ),
        )
        if x == 0:
            total = total + west_u + (west_v - before(west_v, 0)) + (west_w - before(west_w, 1))
        if x == 1:
            total = total - west_u
        if x == last:
            total = total + east_u + (east_v - before(east_v, 0)) + (east_w - before(east_w, 1))
        slab.append(total)
    last_u = along_x[0] + east_u + jnp.where(
        row == 0, south_u[last:], jnp.where(row == plan.sy - 1, north_u[last:], 0.0)
    )
    column = lax.broadcasted_iota(jnp.int32, (plan.sx, plan.nz), 0)
    last_v = along_y[0] + north_v + jnp.where(
        column == 0,
        west_v[plan.sy - 1 :],
        jnp.where(column == last, east_v[plan.sy - 1 :], 0.0),
    )
    tiled_plane = jnp.concatenate([-last_u] * plan.x4, axis=0)
    tiled_rows = []
    for p in range(plan.x4):
        block = jnp.zeros((plan.sy, plan.nz), jnp.float32)
        for g in range(plan.xg):
            at = g * plan.x4 + p
            block = jnp.where(row % plan.xg == g, -last_v[at : at + 1], block)
        tiled_rows.append(block)
    modes = from_left(
        forward[...], jnp.concatenate(slab + [tiled_plane] + tiled_rows, axis=0), turned=True
    )
    for g in range(plan.xg):
        for j in range(plan.per):
            out[pl.ds(j * plan.xg + g, plan.nd, stride=plan.rows1), :] = modes[
                j * plan.nd : (j + 1) * plan.nd, g * LANES : (g + 1) * LANES
            ]
    extra = modes[:, plan.xg * LANES :]
    lane = lax.broadcasted_iota(jnp.int32, (plan.nd, LANES), 1)
    plane_sum = jnp.zeros((plan.nd, LANES), jnp.float32)
    row_sum = jnp.zeros((plan.nd, LANES), jnp.float32)
    for j in range(plan.per):
        part = extra[j * plan.nd : (j + 1) * plan.nd]
        plane_sum = jnp.where(lane // plan.sy == j, part[:, :LANES], plane_sum)
        row_sum = jnp.where(lane % plan.sy // plan.xg == j, part[:, LANES:], row_sum)
    out[pl.ds(plan.main, plan.nd, stride=plan.rows1), :] = plane_sum
    out[pl.ds(plan.main + 1, plan.nd, stride=plan.rows1), :] = row_sum


def regroup(parts, plan):
    group = lax.broadcasted_iota(jnp.int32, parts[0].shape, 1) // plan.sy
    parts = list(parts)
    distance = plan.x4 // 2
    while distance:
        lower = group & distance == 0
        step = distance * plan.sy
        for i in range(plan.x4):
            if not i & distance:
                one, two = parts[i], parts[i + distance]
                parts[i] = jnp.where(lower, one, pltpu.roll(two, step, 1))
                parts[i + distance] = jnp.where(lower, pltpu.roll(one, LANES - step, 1), two)
        distance //= 2
    return parts


def solve_kernel(plan, r, leave, eigen_x, eigen_yz, tables, out):
    wide_x, wide_y = 2 * plan.tx, 2 * plan.ty
    fy, by = tables[0, :wide_y, :wide_y], tables[1, :wide_y, :wide_y]
    fx, bx = tables[2, :wide_x, :wide_x], tables[3, :wide_x, :wide_x]
    rank = lax.axis_index("gx") * plan.gy + lax.axis_index("gy")
    eigen = eigen_x[...] + eigen_yz[pl.ds(rank, 1), :]
    inverse = jnp.where(eigen == 0.0, 0.0, 1.0 / jnp.where(eigen == 0.0, 1.0, eigen))
    gx, gy, per, xg, x4 = plan.gx, plan.gy, plan.per, plan.xg, plan.x4
    lane = lax.broadcasted_iota(jnp.int32, (gx, LANES), 1)
    first_lanes = lane < plan.sy
    first_rows = lane % plan.sy == 0
    step1, step2 = gy * plan.rows1, gy * plan.rows2

    def take(b, q):
        return r[pl.ds(b * plan.rows1 + q, gx, stride=step1), :]

    blocks = [[take(b, q) for q in range(plan.main)] for b in range(gy)]
    for b in range(gy):
        plane = pltpu.roll(take(b, plan.main), 1, 0)
        for j in range(per):
            moved = plane if j == 0 else pltpu.roll(plane, LANES - j * plan.sy, 1)
            blocks[b][j * xg] = blocks[b][j * xg] + jnp.where(first_lanes, moved, 0.0)
        rows = take(b, plan.main + 1)
        for q in range(plan.main):
            moved = rows if q == 0 else pltpu.roll(rows, LANES - q, 1)
            nb = (b + 1) % gy
            blocks[nb][q] = blocks[nb][q] + jnp.where(first_rows, moved, 0.0)
    turned = [
        [regroup([blocks[h + i][q] for i in range(x4)], plan) for h in range(0, gy, x4)]
        for q in range(plan.main)
    ]
    grid = jnp.concatenate(
        [
            jnp.concatenate([part[p] for part in turned[q]], axis=1)
            for p in range(x4)
            for q in range(plan.main)
        ],
        axis=0,
    )
    in_y = from_right(grid, fy)
    height = xg * gx

    def piece(value, row, column):
        return value[row * height : (row + 1) * height, column * plan.ty : (column + 1) * plan.ty]

    in_y = jnp.concatenate(
        [
            jnp.concatenate([piece(in_y, p * per + j, 0) for p in range(x4)], axis=0)
            for j in range(per)
        ],
        axis=1,
    )
    spectrum = from_left(fx, in_y)
    solved = spectrum * inverse
    in_x = from_left(bx, solved)
    in_x = jnp.concatenate([piece(in_x, p, j) for p in range(x4) for j in range(per)], axis=0)
    grid = from_right(in_x, by)
    blocks = [[None] * plan.main for _ in range(gy)]
    for q in range(plan.main):
        for h in range(0, gy, x4):
            parts = [
                grid[
                    (p * plan.main + q) * gx : (p * plan.main + q + 1) * gx,
                    h * plan.sy : h * plan.sy + LANES,
                ]
                for p in range(x4)
            ]
            for i, part in enumerate(regroup(parts, plan)):
                blocks[h + i][q] = part
    scale = 1.0 / (plan.nz * math.sqrt(plan.tx * plan.ty))
    mean = jnp.where(rank == 0, spectrum[0:1, 0:1] * scale, 0.0)
    mean = jnp.where(lane == plan.edge + 3 * per, mean, 0.0)

    def moved(block, source, target):
        return pltpu.roll(jnp.where(lane == source, block, 0.0), (target - source) % LANES, 1)

    for b in range(gy):
        for q in range(plan.main):
            out[pl.ds(b * plan.rows2 + q, gx, stride=step2), :] = blocks[b][q]
        along_x = jnp.zeros((gx, LANES), jnp.float32)
        row = leave[pl.ds(b, gx, stride=gy), :] + mean
        for j in range(per):
            here = blocks[b][j * xg]
            along_x = along_x + moved(here, 0, plan.edge + j)
            along_x = along_x + moved(here, plan.sy - 1, plan.edge + 2 * per + j)
            row = row + moved(blocks[(b + 1) % gy][j * xg], 0, plan.edge + per + j)
        out[pl.ds(b * plan.rows2 + plan.main, gx, stride=step2), :] = row + pltpu.roll(
            along_x, gx - 1, 0
        )


def project_kernel(plan, r, star, stay, backward, place, vel_new, moments):
    nd, per, xg, sy, sx = plan.nd, plan.per, plan.xg, plan.sy, plan.sx
    lane = lax.broadcasted_iota(jnp.int32, (nd, LANES), 1) - plan.edge

    def take(q):
        return r[pl.ds(q, nd, stride=plan.rows2), :]

    row = take(plan.main)
    beyond = (lane >= 0) & (lane < 3 * per)
    beyond = [jnp.where(beyond & (lane % per == j), row, 0.0) for j in range(per)]
    modes = [
        jnp.concatenate([take(j * xg + g) for j in range(per)], axis=0) for g in range(xg)
    ]
    modes.append(jnp.concatenate(beyond, axis=0))
    cells = from_right(jnp.concatenate(modes, axis=1), backward[...], turned=True)

    def cell(k):
        at = xg * LANES + plan.edge + k * per
        return functools.reduce(jnp.add, [cells[at + j : at + j + 1] for j in range(per)])

    east_first, north_first, east_last = cell(0), cell(1), cell(2)
    came = jnp.sum(row, axis=0, keepdims=True)
    mean = came[:, plan.edge + 3 * per : plan.edge + 3 * per + 1]
    pressure = [cells[x * sy : (x + 1) * sy] for x in range(sx)]
    y = lax.broadcasted_iota(jnp.int32, (sy, plan.nz), 0)
    z = lax.broadcasted_iota(jnp.int32, (sy, plan.nz), 1)
    ends = slice(sy - 8, sy)
    u_before = None
    for x in range(sx):
        here = pressure[x]
        upper = jnp.where(z == plan.nz - 1, here, pltpu.roll(here, plan.nz - 1, 1))
        w = star[2, x] - (upper - here)
        along_z = w - before(w, 1)
        v = star[1, x] - (pltpu.roll(here, sy - 1, 0) - here)
        if x < sx - 1:
            u = star[0, x] - (pressure[x + 1] - here)
        else:
            u = u_before - (v - pltpu.roll(v, 1, 0)) - along_z + mean
            u = jnp.where(y == 0, star[0, x] - (east_first - here), u)
            u = jnp.where(y == sy - 1, star[0, x] - (east_last - here), u)
        if x == 0:
            v_last = star[1, x, ends] - (north_first - here[ends])
        else:
            v_last = pltpu.roll(v[ends], 1, 0) - (u[ends] - u_before[ends]) - along_z[ends] + mean
        v_last = jnp.where(y[ends] == sy - 1, v_last, v[ends])
        vel_new[0, x] = u
        vel_new[1, x, : sy - 8] = v[: sy - 8]
        vel_new[1, x, sy - 8 :] = v_last
        vel_new[2, x] = w
        u_before = u
    load = lax.broadcasted_iota(jnp.int32, (8, LANES), 0)
    at = lax.broadcasted_iota(jnp.int32, (8, LANES), 1)
    loads = jnp.where(at // plan.width == load, came, 0.0)
    total = stay[...] + lax.dot_general(
        loads, place[...], NN, precision=lax.Precision.HIGHEST, preferred_element_type=jnp.float32
    )
    moments[...] = total[:3, : plan.boxes] * (1.0 / plan.slots)


def droplet_tables(plan):
    bx, by, boxes = plan.bx, plan.by, plan.boxes
    width = plan.width
    lane_of = {}
    kind_of = np.full((LANES,), -1)
    place = np.zeros((LANES, LANES), np.float32)
    for k, (sx, sy) in enumerate(KINDS):
        xs = range(bx) if sx == 0 else [0 if sx > 0 else bx - 1]
        ys = range(by) if sy == 0 else [0 if sy > 0 else by - 1]
        for x in xs:
            for y in ys:
                lane_of[k, x, y] = len(lane_of)
    assert len(lane_of) == width
    for (k, x, y), at in lane_of.items():
        for load in range(3):
            kind_of[load * width + at] = k
            place[load * width + at, x * by + y] = 1.0
    goes = np.zeros((9 * boxes, LANES), np.float32)
    for dx in (-1, 0, 1):
        for dy in (-1, 0, 1):
            code = (dx + 1) * 3 + dy + 1
            for x in range(bx):
                for y in range(by):
                    line = code * boxes + x * by + y
                    sx = (x + dx) // bx
                    sy = (y + dy) // by
                    tx, ty = (x + dx) % bx, (y + dy) % by
                    if (sx, sy) == (0, 0):
                        goes[line, tx * by + ty] = 1.0
                    else:
                        goes[line, boxes + lane_of[KINDS.index((sx, sy)), tx, ty]] = 1.0
    return goes, place, kind_of[None].astype(np.int32)


def quotient(value, divisor):
    if divisor & (divisor - 1) == 0:
        return value >> (divisor.bit_length() - 1), value & (divisor - 1)
    return lax.div(value, divisor), lax.rem(value, divisor)


def scalar_kernel(
    plan, vel, theta, vapour, xb, yb, xa, ya, radius, multiplicity, counts, pairing,
    destination, goes, kind, star, theta_new, vapour_new, stay, leave, moist,
):
    masks = edge_masks(plan)
    bx, by, boxes = plan.bx, plan.by, plan.boxes
    edges = []
    for f in range(5):
        west, east = side_planes(xa, xb, f)
        south, north = side_rows(ya, yb, f)
        edges.append((west, east, south, north))
    sums = []
    total = None
    for x in range(plan.sx):
        coef = coefficients(vel[0, x], vel[1, x], vel[2, x])
        for f, (west, east, south, north) in enumerate(edges):
            ref = (vel.at[0], vel.at[1], vel.at[2], theta, vapour)[f]
            new = (star.at[0], star.at[1], star.at[2], theta_new, moist)[f]
            moved = advect(
                ref[x],
                ref[x + 1] if x < plan.sx - 1 else east,
                ref[x - 1] if x else west,
                north[x : x + 1], south[x : x + 1], coef, masks, plan,
            )
            if f == 2:
                moved = moved + (TIME_STEP * BUOYANCY) * theta[x]
            new[x] = moved
        total = moved if x % BW == 0 else total + moved
        if x % BW == BW - 1:
            sums.append(jnp.sum(total, axis=1, keepdims=True))
    exact = functools.partial(
        lax.dot_general, dimension_numbers=NN, precision=lax.Precision.HIGHEST,
        preferred_element_type=jnp.float32,
    )
    gather_y = (
        lax.broadcasted_iota(jnp.int32, (by, plan.sy), 1) // BW
        == lax.broadcasted_iota(jnp.int32, (by, plan.sy), 0)
    ).astype(jnp.float32)
    spread_y = (
        lax.broadcasted_iota(jnp.int32, (plan.sy, by), 0) // BW
        == lax.broadcasted_iota(jnp.int32, (plan.sy, by), 1)
    ).astype(jnp.float32)
    means = jnp.concatenate(
        [exact(gather_y, jnp.broadcast_to(s, (plan.sy, LANES))) for s in sums], axis=0
    ) * (1.0 / (BW * BW * plan.nz))
    softplus = jnp.maximum(means, 0.0) + jnp.log(1.0 + jnp.exp(-jnp.abs(means)))
    rank_x, rank_y = lax.axis_index("gx"), lax.axis_index("gy")
    box = lax.broadcasted_iota(jnp.int32, (boxes, plan.slots), 0)
    slot = lax.broadcasted_iota(jnp.int32, (boxes, plan.slots), 1)
    device, local = quotient(destination[...], boxes)
    device_x, device_y = quotient(device, plan.gy)
    local_x, local_y = quotient(local, by)
    source_x, source_y = quotient(box, by)
    offset_x = (device_x - rank_x) * bx + local_x - source_x + (1 + bx * plan.gx)
    offset_y = (device_y - rank_y) * by + local_y - source_y + (1 + by * plan.gy)
    offset_x = quotient(offset_x, bx * plan.gx)[1]
    offset_y = quotient(offset_y, by * plan.gy)[1]
    code = (offset_x * 3 + offset_y).astype(jnp.float32)
    line = lax.broadcasted_iota(jnp.int32, (boxes, boxes), 0)
    used = jnp.where(
        line == lax.broadcasted_iota(jnp.int32, (boxes, boxes), 1), counts[...], 0
    )
    used = jnp.sum(used, axis=1, keepdims=True)
    live = jnp.where(slot < used, multiplicity[...], 0.0)
    half = plan.slots // 2
    order = pairing[...]
    index = jnp.concatenate([order, order[:, half:], order[:, :half]], axis=1)

    def gather(value):
        twice = jnp.concatenate([value, value], axis=1)
        return jnp.take_along_axis(twice, index, axis=1, mode="promise_in_bounds")

    radius_sq, live, code = gather(radius[...]), gather(live), gather(code)
    grown_sq = radius_sq + GROWTH * softplus
    root = jnp.sqrt(grown_sq)
    mass = grown_sq * root
    lane = lax.broadcasted_iota(jnp.int32, (boxes, LANES), 1)
    own = lane < plan.slots
    condensed = jnp.sum(
        jnp.where(own, live * (mass - radius_sq * jnp.sqrt(radius_sq)), 0.0),
        axis=1, keepdims=True,
    )
    condensed = jnp.broadcast_to(condensed, (boxes, LANES))
    for big in range(bx):
        less = CONDENSE * exact(spread_y, condensed[big * by : (big + 1) * by])
        for x in range(big * BW, (big + 1) * BW):
            vapour_new[x] = moist[x] - less

    def partner(value):
        return pltpu.roll(value, LANES - plan.slots, 1)

    other_grown, other_root, other_mass = partner(grown_sq), partner(root), partner(mass)
    both = root + other_root
    rate = both * both * jnp.abs(grown_sq - other_grown) * partner(live)
    final = (mass + COLLISION * rate * other_mass) / (1.0 + COLLISION * rate)
    weight = jnp.where(own, live, 0.0)
    loads = (weight, weight * final, weight * final * final)
    parts = [[], [], []]
    for direction in range(9):
        chosen = code == float(direction)
        for k in range(3):
            parts[k].append(
                jnp.sum(jnp.where(chosen, loads[k], 0.0), axis=1, keepdims=True)
            )
    payload = jnp.zeros((1, LANES), jnp.float32)
    stays = jnp.zeros((8, LANES), jnp.float32)
    line = lax.broadcasted_iota(jnp.int32, (8, LANES), 0)
    lane = lax.broadcasted_iota(jnp.int32, (1, LANES), 1)
    width = plan.width
    leaving = (lane >= boxes) & (lane < boxes + width)
    for k in range(3):
        column = jnp.concatenate(parts[k], axis=0)
        landed = jnp.sum(column * goes[...], axis=0, keepdims=True)
        stays = jnp.where(line == k, landed, stays)
        payload = payload + pltpu.roll(
            jnp.where(leaving, landed, 0.0), (k * width - boxes) % LANES, 1
        )
    stay[...] = stays
    owner = jnp.full((1, LANES), -1, jnp.int32)
    for k, (sx, sy) in enumerate(KINDS):
        to_x = lax.rem(rank_x + (sx + plan.gx), plan.gx)
        to_y = lax.rem(rank_y + (sy + plan.gy), plan.gy)
        owner = jnp.where(kind[...] == k, to_x * plan.gy + to_y, owner)
    every = lax.broadcasted_iota(jnp.int32, (plan.nd, LANES), 0)
    leave[...] = jnp.where(every == owner, payload, 0.0)


def call(body, outs, args, flops, scratch=(), space=VMEM):
    moved = sum(a.size * a.dtype.itemsize for a in args)
    moved += sum(math.prod(o) * 4 for o in outs)
    return pl.pallas_call(
        body,
        out_shape=[jax.ShapeDtypeStruct(o, jnp.float32) for o in outs],
        in_specs=[space] * len(args),
        out_specs=[VMEM] * len(outs),
        scratch_shapes=list(scratch),
        compiler_params=pltpu.CompilerParams(vmem_limit_bytes=16 * 2**20),
        cost_estimate=pl.CostEstimate(flops=flops, bytes_accessed=moved, transcendentals=0),
    )(*args)


def exchange(chunks, plan, rows):
    flat = chunks.reshape(plan.nd, 1, rows * LANES)
    flat = lax.all_to_all(flat, ("gx", "gy"), split_axis=0, concat_axis=0, tiled=True)
    return flat.reshape(plan.nd * rows, LANES)


def shards(velocity, theta, vapour, radius_sq, multiplicity, counts, pairing, destination):
    span_x, span_y, levels = theta.shape
    slots = radius_sq.shape[0]
    plan = Plan(lax.axis_size("gx"), lax.axis_size("gy"), span_x, span_y, levels, slots)
    forward, backward, q1, qy, ex, ey, ez = plan.tables()
    goes, place, kind = droplet_tables(plan)
    block = (span_x, span_y, levels)
    cells = math.prod(block)

    plane, rows = (5, span_y, levels), (5, span_x, levels)
    fields = (velocity, theta, vapour)
    placed = [pltpu.with_memory_space_constraint(f, pltpu.HBM) for f in fields]
    xb, xa = call(
        functools.partial(planes_kernel, plan), (plane, plane), placed, cells,
        [pltpu.SemaphoreType.DMA((2, 3))], HBM,
    )
    yb, ya = call(functools.partial(rows_kernel, plan), (rows, rows), (*fields, xa), cells)
    ways_x, ways_y = neighbours(plan.gx), neighbours(plan.gy)
    xb, xa = lax.ppermute(xb, "gx", ways_x[1]), lax.ppermute(xa, "gx", ways_x[0])
    yb, ya = lax.ppermute(yb, "gy", ways_y[1]), lax.ppermute(ya, "gy", ways_y[0])
    halo = (xb, yb, xa, ya)

    inner = call(
        functools.partial(inner_kernel, plan),
        (block, (3, span_y, levels), (3, span_x, levels)), (velocity, theta), 100 * cells,
    )
    (chunks,) = call(
        functools.partial(spread_kernel, plan), ((plan.nd * plan.rows1, LANES),),
        (*inner, *halo, on_left(forward)), 100 * cells,
    )
    spectral = exchange(chunks, plan, plan.rows1)

    tables = [on_right(qy), on_right(qy.T), on_left(q1), on_left(q1.T)]
    most = max(t.shape[0] for t in tables)
    tables = np.stack([np.pad(t, (0, most - t.shape[0])) for t in tables])
    eigen_x = ex.astype(np.float32)[:, None]
    eigen_yz = (ez.reshape(plan.nd, plan.per, 1) + ey).reshape(plan.nd, -1).astype(np.float32)
    star, theta_new, vapour_new, stay, leave = call(
        functools.partial(scalar_kernel, plan),
        ((3,) + block, block, block, (8, LANES), (plan.nd, LANES)),
        fields + halo + (radius_sq.T, multiplicity.T, counts[None], pairing)
        + (destination.T, goes, kind),
        100 * cells,
        (pltpu.VMEM(block, jnp.float32),),
    )

    (chunks,) = call(
        functools.partial(solve_kernel, plan),
        ((plan.nd * plan.rows2, LANES),),
        (spectral, leave, eigen_x, eigen_yz, tables),
        1000 * cells,
    )
    modal = exchange(chunks, plan, plan.rows2)

    velocity_new, moments = call(
        functools.partial(project_kernel, plan),
        ((3,) + block, (3, plan.boxes)),
        (modal, star, stay, on_right(backward), place),
        100 * cells,
    )
    return (velocity_new, theta_new, vapour_new, moments)


def solution(mesh):
    placed = (
        P(None, "gx", "gy", None),
        P("gx", "gy", None),
        P("gx", "gy", None),
        P(None, ("gx", "gy")),
        P(None, ("gx", "gy")),
        P(("gx", "gy")),
        P(("gx", "gy"), None),
        P(None, ("gx", "gy")),
    )
    return jax.shard_map(
        shards,
        mesh=mesh,
        in_specs=placed,
        out_specs=(
            P(None, "gx", "gy", None),
            P("gx", "gy", None),
            P("gx", "gy", None),
            P(None, ("gx", "gy")),
        ),
        check_vma=False,
    )
```

```python
import functools
import math

import jax
import jax.numpy as jnp
import ml_dtypes
import numpy as np
from jax import lax
from jax.experimental import pallas as pl
from jax.experimental.pallas import tpu as pltpu
from jax.sharding import PartitionSpec as P

BW = 4
LANES = 128

TIME_STEP = 0.2
DIFFUSION = 0.05
BUOYANCY = 0.5
GROWTH = 0.5
COLLISION = 0.05
CONDENSE = 0.002

VMEM = pl.BlockSpec(memory_space=pltpu.VMEM)
HBM = pl.BlockSpec(memory_space=pltpu.HBM)
NT = (((1,), (1,)), ((), ()))
TN = (((0,), (0,)), ((), ()))
NN = (((1,), (0,)), ((), ()))

KINDS = [(sx, sy) for sx in (-1, 0, 1) for sy in (-1, 0, 1) if (sx, sy) != (0, 0)]


def halves(table):
    high = table.astype(np.float32).astype(ml_dtypes.bfloat16)
    low = (table - high.astype(np.float64)).astype(np.float32).astype(ml_dtypes.bfloat16)
    return np.concatenate([high, low], axis=0)


def on_left(pair):
    return jnp.concatenate([pair, pair], axis=1)


def on_right(pair):
    size = pair.shape[0] // 2
    once = jnp.concatenate([pair[:size], pair[size:]], axis=1)
    return jnp.concatenate([once, once], axis=0)


def split(value, axis):
    high = value.astype(jnp.bfloat16)
    low = (value - high.astype(jnp.float32)).astype(jnp.bfloat16)
    return jnp.concatenate([high, low], axis=axis)


def from_left(table, value, turned=False):
    out = lax.dot_general(
        table, split(value, 1 if turned else 0), NT if turned else NN,
        preferred_element_type=jnp.float32,
    )
    rows = out.shape[0] // 2
    return out[:rows] + out[rows:]


def from_right(value, table, turned=False):
    out = lax.dot_general(
        split(value, 0 if turned else 1), table, TN if turned else NN,
        preferred_element_type=jnp.float32,
    )
    columns = out.shape[1] // 2
    return out[:, :columns] + out[:, columns:]


def real_basis(length):
    position = np.arange(length)[:, None]
    column = np.arange(length)
    wave = np.where(column <= length // 2, column, column - length // 2)
    angle = 2.0 * np.pi * ((position * wave[None, :]) % length) / length
    table = np.where(column[None, :] <= length // 2, np.cos(angle), np.sin(angle))
    table = table * np.sqrt(2.0 / length)
    table[:, 0] *= np.sqrt(0.5)
    if length % 2 == 0:
        table[:, length // 2] *= np.sqrt(0.5)
    return table, -4.0 * np.sin(np.pi * wave / length) ** 2


class Plan:
    def __init__(self, grid_x, grid_y, span_x, span_y, levels, slots):
        self.gx, self.gy = grid_x, grid_y
        self.sx, self.sy, self.nz = span_x, span_y, levels
        self.nd = grid_x * grid_y
        self.per = levels // self.nd
        self.x4 = LANES // span_y
        self.xg = span_x // self.x4
        self.main = self.per * self.xg
        self.rows1 = self.main + 1
        self.rows2 = self.main + 1
        self.tx, self.ty = grid_x * span_x, grid_y * span_y
        self.bx, self.by = span_x // BW, span_y // BW
        self.boxes = self.bx * self.by
        self.slots = slots
        self.width = 2 * self.by + 2 * self.bx + 4
        self.edge = 3 * self.width
        assert max(self.edge + 3 * self.per + 1, self.boxes + self.width) <= LANES

    def tables(self):
        nd, per, nz = self.nd, self.per, self.nz
        z = np.arange(nz)
        cosine = np.cos(np.pi / nz * (((2 * z[:, None] + 1) * z[None, :]) % (4 * nz)) / 2.0)
        mode = (np.arange(nd)[None, :] * per + np.arange(per)[:, None]).reshape(-1)
        forward = cosine.T[mode]
        weight = np.where(np.arange(nz) == 0, 1.0, 2.0) / nz
        backward = forward * weight[mode][:, None]
        qx, ex = real_basis(self.tx)
        qy, ey = real_basis(self.ty)
        q1 = qx.reshape(self.gx, self.xg, self.x4, self.tx)
        q1 = q1.transpose(3, 2, 1, 0).reshape(self.tx, self.tx)
        ez = -4.0 * np.sin(np.pi * z / (2 * nz)) ** 2
        return forward, backward, q1, qy, ex, ey, ez


def neighbours(count):
    first = [(i, i ^ 1) for i in range(count)]
    second = [(i, (i + 1) % count if i % 2 else (i - 1) % count) for i in range(count)]
    return first, second


def copy_all(copies):
    for copy in copies:
        copy.start()
    for copy in copies:
        copy.wait()


def planes_kernel(plan, vel, theta, vapour, xb, xa, sems):
    odd = lax.axis_index("gx") % 2
    copies = []
    for side, (out, x) in enumerate(((xb, odd), (xa, 1 - odd))):
        second = 1 + x * (plan.sx - 3)
        x = x * (plan.sx - 1)
        copies += [
            pltpu.make_async_copy(vel.at[0, second], out.at[5], sems.at[side, 3]),
            pltpu.make_async_copy(vel.at[:, x], out.at[0:3], sems.at[side, 0]),
            pltpu.make_async_copy(theta.at[x], out.at[3], sems.at[side, 1]),
            pltpu.make_async_copy(vapour.at[x], out.at[4], sems.at[side, 2]),
        ]
    for copy in copies:
        copy.start()
    for copy in copies:
        copy.wait()


def rows_kernel(plan, vel, theta, vapour, after, yb, ya):
    odd = lax.axis_index("gy") % 2 == 1
    for f, ref in enumerate((vel.at[0], vel.at[1], vel.at[2], theta, vapour)):
        for x in range(plan.sx):
            low, high = ref[x, 0:1], ref[x, plan.sy - 1 :]
            ya[f, x : x + 1] = jnp.where(odd, low, high)
            yb[f, x : x + 1] = jnp.where(odd, high, low)
    for x in range(plan.sx):
        low, high = vel[1, x, 1:2], vel[1, x, plan.sy - 2 : plan.sy - 1]
        ya[5, x : x + 1] = jnp.where(odd, low, high)
        yb[5, x : x + 1] = jnp.where(odd, high, low)


def edge_masks(plan):
    row = lax.broadcasted_iota(jnp.int32, (plan.sy, plan.nz), 0)
    lane = lax.broadcasted_iota(jnp.int32, (plan.sy, plan.nz), 1)
    return row == 0, row == plan.sy - 1, lane == 0, lane == plan.nz - 1


def coefficients(u, v, w):
    half = 0.5 * TIME_STEP
    side = TIME_STEP * DIFFUSION
    return (
        side - half * u, side + half * u,
        side - half * v, side + half * v,
        side - half * w, side + half * w,
    )


def advect(c, east, west, north_row, south_row, coef, masks, plan):
    row0, row_last, lane0, lane_last = masks
    north = jnp.where(row_last, north_row, pltpu.roll(c, plan.sy - 1, 0))
    south = jnp.where(row0, south_row, pltpu.roll(c, 1, 0))
    return weigh(c, east, west, north, south, coef, lane0, lane_last)


def weigh(c, east, west, north, south, coef, lane0, lane_last):
    upper = jnp.where(lane_last, c, pltpu.roll(c, c.shape[1] - 1, 1))
    lower = jnp.where(lane0, c, pltpu.roll(c, 1, 1))
    ce, cw, cn, cs, cu, cl = coef
    return (
        (1.0 - 6.0 * TIME_STEP * DIFFUSION) * c
        + (ce * east + cw * west)
        + (cn * north + cs * south)
        + (cu * upper + cl * lower)
    )


def side_planes(xa, xb, f):
    odd = lax.axis_index("gx") % 2 == 1
    return jnp.where(odd, xa[f], xb[f]), jnp.where(odd, xb[f], xa[f])


def side_rows(ya, yb, f):
    odd = lax.axis_index("gy") % 2 == 1
    return jnp.where(odd, ya[f], yb[f]), jnp.where(odd, yb[f], ya[f])


def before(value, axis):
    at = lax.broadcasted_iota(jnp.int32, value.shape, axis)
    return jnp.where(at == 0, 0.0, pltpu.roll(value, 1, axis))


def inner_kernel(plan, vel, theta, div, along_x, along_y):
    masks = edge_masks(plan)
    zero = jnp.zeros((plan.sy, plan.nz), jnp.float32)
    zero_row = jnp.zeros((1, plan.nz), jnp.float32)
    last = plan.sx - 1
    last_u = None
    for x in range(plan.sx):
        coef = coefficients(vel[0, x], vel[1, x], vel[2, x])
        u, v, w = (
            advect(
                vel[f, x],
                vel[f, x + 1] if x < last else zero,
                vel[f, x - 1] if x else zero,
                zero_row, zero_row, coef, masks, plan,
            )
            for f in range(3)
        )
        w = w + (TIME_STEP * BUOYANCY) * theta[x]
        total = (u if last_u is None else u - last_u) + (v - before(v, 0)) + (w - before(w, 1))
        div[x] = total
        last_u = u
        along_y[0, x : x + 1] = v[plan.sy - 1 : plan.sy]
        along_y[1, x : x + 1] = coef[3][0:1]
        along_y[2, x : x + 1] = coef[2][plan.sy - 1 : plan.sy]
        along_y[3, x : x + 1] = vel[1, x, 0:1]
        if x == 0:
            along_x[1] = coef[1]
            along_x[3] = vel[0, x]
        if x == last:
            along_x[0] = u
            along_x[2] = coef[0]


def spread_kernel(plan, div, along_x, along_y, xb, yb, xa, ya, forward, out):
    sides = [side_planes(xa, xb, f) for f in range(3)]
    ends = [side_rows(ya, yb, f) for f in range(3)]
    west_u, west_v, west_w = (along_x[1] * west for west, _ in sides)
    east_u, east_v, east_w = (along_x[2] * east for _, east in sides)
    south_u, south_v, south_w = (along_y[1] * south for south, _ in ends)
    north_u, north_v, north_w = (along_y[2] * north for _, north in ends)
    first_row = south_u - before(south_u, 0) + south_v + south_w - before(south_w, 1)
    last_row = north_u - before(north_u, 0) + north_v + north_w - before(north_w, 1)
    row = lax.broadcasted_iota(jnp.int32, (plan.sy, plan.nz), 0)
    column = lax.broadcasted_iota(jnp.int32, (plan.sx, plan.nz), 0)
    level = lax.broadcasted_iota(jnp.int32, (plan.sx, plan.nz), 1)
    last = plan.sx - 1
    west = [side[0] for side in sides]
    none = jnp.zeros((1, plan.nz), jnp.float32)
    west_star = advect(
        west[0], along_x[3], side_planes(xa, xb, 5)[0], none, none, coefficients(*west),
        edge_masks(plan), plan,
    )
    south = [end[0] for end in ends]
    south_star = weigh(
        south[1],
        jnp.where(column == last, 0.0, pltpu.roll(south[1], plan.sx - 1, 0)),
        before(south[1], 0),
        along_y[3],
        side_rows(ya, yb, 5)[0],
        coefficients(*south),
        level == 0,
        level == plan.nz - 1,
    )
    first_row = first_row - south_star
    slab = []
    for x in range(plan.sx):
        at = slice(x, x + 1)
        total = div[x] + jnp.where(
            row == 0,
            first_row[at],
            jnp.where(
                row == 1, -south_v[at], jnp.where(row == plan.sy - 1, last_row[at], 0.0)
            ),
        )
        if x == 0:
            total = total - west_star + west_u + (west_v - before(west_v, 0)) + (west_w - before(west_w, 1))
        if x == 1:
            total = total - west_u
        if x == last:
            total = total + east_u + (east_v - before(east_v, 0)) + (east_w - before(east_w, 1))
        slab.append(total)
    corners = (
        south_u[last:], north_u[last:], west_v[plan.sy - 1 :], east_v[plan.sy - 1 :]
    )
    block = jnp.zeros((plan.sy, plan.nz), jnp.float32)
    for k, corner in enumerate(corners):
        block = jnp.where(row == k, -corner, block)
    modes = from_left(
        on_left(forward[...]), jnp.concatenate(slab + [block] * plan.x4, axis=0), turned=True
    )
    for g in range(plan.xg):
        for j in range(plan.per):
            out[pl.ds(j * plan.xg + g, plan.nd, stride=plan.rows1), :] = modes[
                j * plan.nd : (j + 1) * plan.nd, g * LANES : (g + 1) * LANES
            ]
    extra = modes[:, plan.xg * LANES :]
    lane = lax.broadcasted_iota(jnp.int32, (plan.nd, LANES), 1)
    total = jnp.zeros((plan.nd, LANES), jnp.float32)
    for j in range(plan.per):
        part = extra[j * plan.nd : (j + 1) * plan.nd]
        total = jnp.where(lane // plan.sy == j, part, total)
    out[pl.ds(plan.main, plan.nd, stride=plan.rows1), :] = total


def regroup(parts, plan):
    group = lax.broadcasted_iota(jnp.int32, parts[0].shape, 1) // plan.sy
    parts = list(parts)
    distance = plan.x4 // 2
    while distance:
        lower = group & distance == 0
        step = distance * plan.sy
        for i in range(plan.x4):
            if not i & distance:
                one, two = parts[i], parts[i + distance]
                parts[i] = jnp.where(lower, one, pltpu.roll(two, step, 1))
                parts[i + distance] = jnp.where(lower, pltpu.roll(one, LANES - step, 1), two)
        distance //= 2
    return parts


def solve_kernel(plan, r, leave, eigen_x, eigen_yz, tables, out):
    wide_x, wide_y = 2 * plan.tx, 2 * plan.ty
    fy, by = (on_right(tables[i, :wide_y, : plan.ty]) for i in (0, 1))
    fx, bx = (on_left(tables[i, :wide_x, : plan.tx]) for i in (2, 3))
    rank = lax.axis_index("gx") * plan.gy + lax.axis_index("gy")
    eigen = eigen_x[...] + eigen_yz[pl.ds(rank, 1), :]
    inverse = jnp.where(eigen == 0.0, 0.0, 1.0 / jnp.where(eigen == 0.0, 1.0, eigen))
    gx, gy, per, xg, x4 = plan.gx, plan.gy, plan.per, plan.xg, plan.x4
    lane = lax.broadcasted_iota(jnp.int32, (gx, LANES), 1)
    step1, step2 = gy * plan.rows1, gy * plan.rows2

    def take(b, q):
        return r[pl.ds(b * plan.rows1 + q, gx, stride=step1), :]

    def moved(block, source, target):
        return pltpu.roll(jnp.where(lane == source, block, 0.0), (target - source) % LANES, 1)

    blocks = [[take(b, q) for q in range(plan.main)] for b in range(gy)]
    for b in range(gy):
        here = take(b, plan.main)
        ahead = pltpu.roll(here, 1, 0)
        nb = (b + 1) % gy
        for j in range(per):
            at, first, final = j * plan.sy, j * xg, j * xg + xg - 1
            blocks[b][first] = blocks[b][first] + (
                moved(ahead, at, 0) + moved(ahead, at + 1, plan.sy - 1)
            )
            blocks[nb][first] = blocks[nb][first] + moved(here, at + 2, 0)
            blocks[nb][final] = blocks[nb][final] + moved(here, at + 3, (x4 - 1) * plan.sy)
    turned = [
        [regroup([blocks[h + i][q] for i in range(x4)], plan) for h in range(0, gy, x4)]
        for q in range(plan.main)
    ]
    grid = jnp.concatenate(
        [
            jnp.concatenate([part[p] for part in turned[q]], axis=1)
            for p in range(x4)
            for q in range(plan.main)
        ],
        axis=0,
    )
    in_y = from_right(grid, fy)
    height = xg * gx

    def piece(value, row, column):
        return value[row * height : (row + 1) * height, column * plan.ty : (column + 1) * plan.ty]

    in_y = jnp.concatenate(
        [
            jnp.concatenate([piece(in_y, p * per + j, 0) for p in range(x4)], axis=0)
            for j in range(per)
        ],
        axis=1,
    )
    spectrum = from_left(fx, in_y)
    solved = spectrum * inverse
    in_x = from_left(bx, solved)
    in_x = jnp.concatenate([piece(in_x, p, j) for p in range(x4) for j in range(per)], axis=0)
    grid = from_right(in_x, by)
    blocks = [[None] * plan.main for _ in range(gy)]
    for q in range(plan.main):
        for h in range(0, gy, x4):
            parts = [
                grid[
                    (p * plan.main + q) * gx : (p * plan.main + q + 1) * gx,
                    h * plan.sy : h * plan.sy + LANES,
                ]
                for p in range(x4)
            ]
            for i, part in enumerate(regroup(parts, plan)):
                blocks[h + i][q] = part
    scale = 1.0 / (plan.nz * math.sqrt(plan.tx * plan.ty))
    mean = jnp.where(rank == 0, spectrum[0:1, 0:1] * scale, 0.0)
    mean = jnp.where(lane == plan.edge + 3 * per, mean, 0.0)

    for b in range(gy):
        for q in range(plan.main):
            out[pl.ds(b * plan.rows2 + q, gx, stride=step2), :] = blocks[b][q]
        along_x = jnp.zeros((gx, LANES), jnp.float32)
        row = leave[pl.ds(b, gx, stride=gy), :] + mean
        for j in range(per):
            here = blocks[b][j * xg]
            along_x = along_x + moved(here, 0, plan.edge + j)
            along_x = along_x + moved(here, plan.sy - 1, plan.edge + 2 * per + j)
            row = row + moved(blocks[(b + 1) % gy][j * xg], 0, plan.edge + per + j)
        out[pl.ds(b * plan.rows2 + plan.main, gx, stride=step2), :] = row + pltpu.roll(
            along_x, gx - 1, 0
        )


def project_kernel(plan, r, star, stay, backward, place, vel_new, moments):
    nd, per, xg, sy, sx = plan.nd, plan.per, plan.xg, plan.sy, plan.sx
    lane = lax.broadcasted_iota(jnp.int32, (nd, LANES), 1) - plan.edge

    def take(q):
        return r[pl.ds(q, nd, stride=plan.rows2), :]

    row = take(plan.main)
    beyond = (lane >= 0) & (lane < 3 * per)
    beyond = [jnp.where(beyond & (lane % per == j), row, 0.0) for j in range(per)]
    modes = [
        jnp.concatenate([take(j * xg + g) for j in range(per)], axis=0) for g in range(xg)
    ]
    modes.append(jnp.concatenate(beyond, axis=0))
    cells = from_right(jnp.concatenate(modes, axis=1), on_right(backward[...]), turned=True)

    def cell(k):
        at = xg * LANES + plan.edge + k * per
        return functools.reduce(jnp.add, [cells[at + j : at + j + 1] for j in range(per)])

    east_first, north_first, east_last = cell(0), cell(1), cell(2)
    came = jnp.sum(row, axis=0, keepdims=True)
    mean = came[:, plan.edge + 3 * per : plan.edge + 3 * per + 1]
    pressure = [cells[x * sy : (x + 1) * sy] for x in range(sx)]
    y = lax.broadcasted_iota(jnp.int32, (sy, plan.nz), 0)
    z = lax.broadcasted_iota(jnp.int32, (sy, plan.nz), 1)
    ends = slice(sy - 8, sy)
    u_before = None
    for x in range(sx):
        here = pressure[x]
        upper = jnp.where(z == plan.nz - 1, here, pltpu.roll(here, plan.nz - 1, 1))
        w = star[2, x] - (upper - here)
        along_z = w - before(w, 1)
        v = star[1, x] - (pltpu.roll(here, sy - 1, 0) - here)
        if x < sx - 1:
            u = star[0, x] - (pressure[x + 1] - here)
        else:
            u = u_before - (v - pltpu.roll(v, 1, 0)) - along_z + mean
            u = jnp.where(y == 0, star[0, x] - (east_first - here), u)
            u = jnp.where(y == sy - 1, star[0, x] - (east_last - here), u)
        if x == 0:
            v_last = star[1, x, ends] - (north_first - here[ends])
        else:
            v_last = pltpu.roll(v[ends], 1, 0) - (u[ends] - u_before[ends]) - along_z[ends] + mean
        v_last = jnp.where(y[ends] == sy - 1, v_last, v[ends])
        vel_new[0, x] = u
        vel_new[1, x, : sy - 8] = v[: sy - 8]
        vel_new[1, x, sy - 8 :] = v_last
        vel_new[2, x] = w
        u_before = u
    load = lax.broadcasted_iota(jnp.int32, (8, LANES), 0)
    at = lax.broadcasted_iota(jnp.int32, (8, LANES), 1)
    loads = jnp.where(at // plan.width == load, came, 0.0)
    total = stay[...] + lax.dot_general(
        loads, place[...], NN, precision=lax.Precision.HIGHEST, preferred_element_type=jnp.float32
    )
    moments[...] = total[:3, : plan.boxes] * (1.0 / plan.slots)


def droplet_tables(plan):
    bx, by, boxes = plan.bx, plan.by, plan.boxes
    width = plan.width
    lane_of = {}
    kind_of = np.full((LANES,), -1)
    place = np.zeros((LANES, LANES), np.float32)
    for k, (sx, sy) in enumerate(KINDS):
        xs = range(bx) if sx == 0 else [0 if sx > 0 else bx - 1]
        ys = range(by) if sy == 0 else [0 if sy > 0 else by - 1]
        for x in xs:
            for y in ys:
                lane_of[k, x, y] = len(lane_of)
    assert len(lane_of) == width
    for (k, x, y), at in lane_of.items():
        for load in range(3):
            kind_of[load * width + at] = k
            place[load * width + at, x * by + y] = 1.0
    goes = np.zeros((9 * boxes, LANES), np.float32)
    for dx in (-1, 0, 1):
        for dy in (-1, 0, 1):
            code = (dx + 1) * 3 + dy + 1
            for x in range(bx):
                for y in range(by):
                    line = code * boxes + x * by + y
                    sx = (x + dx) // bx
                    sy = (y + dy) // by
                    tx, ty = (x + dx) % bx, (y + dy) % by
                    if (sx, sy) == (0, 0):
                        goes[line, tx * by + ty] = 1.0
                    else:
                        goes[line, boxes + lane_of[KINDS.index((sx, sy)), tx, ty]] = 1.0
    return goes, place, kind_of[None].astype(np.int32)


def quotient(value, divisor):
    if divisor & (divisor - 1) == 0:
        return value >> (divisor.bit_length() - 1), value & (divisor - 1)
    return lax.div(value, divisor), lax.rem(value, divisor)


def scalar_kernel(
    plan, vel, theta, vapour, xb, yb, xa, ya, radius, multiplicity, counts, pairing,
    destination, goes, kind, star, theta_new, vapour_new, stay, leave, moist,
):
    masks = edge_masks(plan)
    bx, by, boxes = plan.bx, plan.by, plan.boxes
    edges = []
    for f in range(5):
        west, east = side_planes(xa, xb, f)
        south, north = side_rows(ya, yb, f)
        edges.append((west, east, south, north))
    sums = []
    total = None
    for x in range(plan.sx):
        coef = coefficients(vel[0, x], vel[1, x], vel[2, x])
        for f, (west, east, south, north) in enumerate(edges):
            ref = (vel.at[0], vel.at[1], vel.at[2], theta, vapour)[f]
            new = (star.at[0], star.at[1], star.at[2], theta_new, moist)[f]
            moved = advect(
                ref[x],
                ref[x + 1] if x < plan.sx - 1 else east,
                ref[x - 1] if x else west,
                north[x : x + 1], south[x : x + 1], coef, masks, plan,
            )
            if f == 2:
                moved = moved + (TIME_STEP * BUOYANCY) * theta[x]
            new[x] = moved
        total = moved if x % BW == 0 else total + moved
        if x % BW == BW - 1:
            sums.append(jnp.sum(total, axis=1, keepdims=True))
    exact = functools.partial(
        lax.dot_general, dimension_numbers=NN, precision=lax.Precision.HIGHEST,
        preferred_element_type=jnp.float32,
    )
    gather_y = (
        lax.broadcasted_iota(jnp.int32, (by, plan.sy), 1) // BW
        == lax.broadcasted_iota(jnp.int32, (by, plan.sy), 0)
    ).astype(jnp.float32)
    spread_y = (
        lax.broadcasted_iota(jnp.int32, (plan.sy, by), 0) // BW
        == lax.broadcasted_iota(jnp.int32, (plan.sy, by), 1)
    ).astype(jnp.float32)
    means = jnp.concatenate(
        [exact(gather_y, jnp.broadcast_to(s, (plan.sy, LANES))) for s in sums], axis=0
    ) * (1.0 / (BW * BW * plan.nz))
    softplus = jnp.maximum(means, 0.0) + jnp.log(1.0 + jnp.exp(-jnp.abs(means)))
    rank_x, rank_y = lax.axis_index("gx"), lax.axis_index("gy")
    box = lax.broadcasted_iota(jnp.int32, (boxes, plan.slots), 0)
    slot = lax.broadcasted_iota(jnp.int32, (boxes, plan.slots), 1)
    device, local = quotient(destination[...], boxes)
    device_x, device_y = quotient(device, plan.gy)
    local_x, local_y = quotient(local, by)
    source_x, source_y = quotient(box, by)
    offset_x = (device_x - rank_x) * bx + local_x - source_x + (1 + bx * plan.gx)
    offset_y = (device_y - rank_y) * by + local_y - source_y + (1 + by * plan.gy)
    offset_x = quotient(offset_x, bx * plan.gx)[1]
    offset_y = quotient(offset_y, by * plan.gy)[1]
    code = (offset_x * 3 + offset_y).astype(jnp.float32)
    line = lax.broadcasted_iota(jnp.int32, (boxes, boxes), 0)
    used = jnp.where(
        line == lax.broadcasted_iota(jnp.int32, (boxes, boxes), 1), counts[...], 0
    )
    used = jnp.sum(used, axis=1, keepdims=True)
    live = jnp.where(slot < used, multiplicity[...], 0.0)
    half = plan.slots // 2
    order = pairing[...]
    index = jnp.concatenate([order, order[:, half:], order[:, :half]], axis=1)

    def gather(value):
        twice = jnp.concatenate([value, value], axis=1)
        return jnp.take_along_axis(twice, index, axis=1, mode="promise_in_bounds")

    radius_sq, live, code = gather(radius[...]), gather(live), gather(code)
    grown_sq = radius_sq + GROWTH * softplus
    root = jnp.sqrt(grown_sq)
    mass = grown_sq * root
    lane = lax.broadcasted_iota(jnp.int32, (boxes, LANES), 1)
    own = lane < plan.slots
    condensed = jnp.sum(
        jnp.where(own, live * (mass - radius_sq * jnp.sqrt(radius_sq)), 0.0),
        axis=1, keepdims=True,
    )
    condensed = jnp.broadcast_to(condensed, (boxes, LANES))
    for big in range(bx):
        less = CONDENSE * exact(spread_y, condensed[big * by : (big + 1) * by])
        for x in range(big * BW, (big + 1) * BW):
            vapour_new[x] = moist[x] - less

    def partner(value):
        return pltpu.roll(value, LANES - plan.slots, 1)

    other_grown, other_root, other_mass = partner(grown_sq), partner(root), partner(mass)
    both = root + other_root
    rate = both * both * jnp.abs(grown_sq - other_grown) * partner(live)
    final = (mass + COLLISION * rate * other_mass) / (1.0 + COLLISION * rate)
    weight = jnp.where(own, live, 0.0)
    loads = (weight, weight * final, weight * final * final)
    parts = [[], [], []]
    for direction in range(9):
        chosen = code == float(direction)
        for k in range(3):
            parts[k].append(
                jnp.sum(jnp.where(chosen, loads[k], 0.0), axis=1, keepdims=True)
            )
    payload = jnp.zeros((1, LANES), jnp.float32)
    stays = jnp.zeros((8, LANES), jnp.float32)
    line = lax.broadcasted_iota(jnp.int32, (8, LANES), 0)
    lane = lax.broadcasted_iota(jnp.int32, (1, LANES), 1)
    width = plan.width
    leaving = (lane >= boxes) & (lane < boxes + width)
    for k in range(3):
        column = jnp.concatenate(parts[k], axis=0)
        landed = jnp.sum(column * goes[...], axis=0, keepdims=True)
        stays = jnp.where(line == k, landed, stays)
        payload = payload + pltpu.roll(
            jnp.where(leaving, landed, 0.0), (k * width - boxes) % LANES, 1
        )
    stay[...] = stays
    owner = jnp.full((1, LANES), -1, jnp.int32)
    for k, (sx, sy) in enumerate(KINDS):
        to_x = lax.rem(rank_x + (sx + plan.gx), plan.gx)
        to_y = lax.rem(rank_y + (sy + plan.gy), plan.gy)
        owner = jnp.where(kind[...] == k, to_x * plan.gy + to_y, owner)
    every = lax.broadcasted_iota(jnp.int32, (plan.nd, LANES), 0)
    leave[...] = jnp.where(every == owner, payload, 0.0)


def call(body, outs, args, flops, scratch=(), space=VMEM):
    moved = sum(a.size * a.dtype.itemsize for a in args)
    moved += sum(math.prod(o) * 4 for o in outs)
    return pl.pallas_call(
        body,
        out_shape=[jax.ShapeDtypeStruct(o, jnp.float32) for o in outs],
        in_specs=[space] * len(args),
        out_specs=[VMEM] * len(outs),
        scratch_shapes=list(scratch),
        compiler_params=pltpu.CompilerParams(vmem_limit_bytes=16 * 2**20),
        cost_estimate=pl.CostEstimate(flops=flops, bytes_accessed=moved, transcendentals=0),
    )(*args)


def exchange(chunks, plan, rows):
    flat = chunks.reshape(plan.nd, 1, rows * LANES)
    flat = lax.all_to_all(flat, ("gx", "gy"), split_axis=0, concat_axis=0, tiled=True)
    return flat.reshape(plan.nd * rows, LANES)


def shards(velocity, theta, vapour, radius_sq, multiplicity, counts, pairing, destination):
    span_x, span_y, levels = theta.shape
    slots = radius_sq.shape[0]
    plan = Plan(lax.axis_size("gx"), lax.axis_size("gy"), span_x, span_y, levels, slots)
    forward, backward, q1, qy, ex, ey, ez = plan.tables()
    goes, place, kind = droplet_tables(plan)
    block = (span_x, span_y, levels)
    cells = math.prod(block)

    plane, rows = (6, span_y, levels), (6, span_x, levels)
    fields = (velocity, theta, vapour)
    placed = [pltpu.with_memory_space_constraint(f, pltpu.HBM) for f in fields]
    xb, xa = call(
        functools.partial(planes_kernel, plan), (plane, plane), placed, cells,
        [pltpu.SemaphoreType.DMA((2, 4))], HBM,
    )
    yb, ya = call(functools.partial(rows_kernel, plan), (rows, rows), (*fields, xa), cells)
    ways_x, ways_y = neighbours(plan.gx), neighbours(plan.gy)
    xb, xa = lax.ppermute(xb, "gx", ways_x[1]), lax.ppermute(xa, "gx", ways_x[0])
    yb, ya = lax.ppermute(yb, "gy", ways_y[1]), lax.ppermute(ya, "gy", ways_y[0])
    halo = (xb, yb, xa, ya)

    inner = call(
        functools.partial(inner_kernel, plan),
        (block, (4, span_y, levels), (4, span_x, levels)), (velocity, theta), 100 * cells,
    )
    (chunks,) = call(
        functools.partial(spread_kernel, plan), ((plan.nd * plan.rows1, LANES),),
        (*inner, *halo, halves(forward)), 100 * cells,
    )
    spectral = exchange(chunks, plan, plan.rows1)

    tables = [halves(qy), halves(qy.T), halves(q1), halves(q1.T)]
    rows, columns = (max(t.shape[i] for t in tables) for i in (0, 1))
    tables = np.stack(
        [np.pad(t, ((0, rows - t.shape[0]), (0, columns - t.shape[1]))) for t in tables]
    )
    eigen_x = ex.astype(np.float32)[:, None]
    eigen_yz = (ez.reshape(plan.nd, plan.per, 1) + ey).reshape(plan.nd, -1).astype(np.float32)
    star, theta_new, vapour_new, stay, leave = call(
        functools.partial(scalar_kernel, plan),
        ((3,) + block, block, block, (8, LANES), (plan.nd, LANES)),
        fields + halo + (radius_sq.T, multiplicity.T, counts[None], pairing)
        + (destination.T, goes, kind),
        100 * cells,
        (pltpu.VMEM(block, jnp.float32),),
    )

    (chunks,) = call(
        functools.partial(solve_kernel, plan),
        ((plan.nd * plan.rows2, LANES),),
        (spectral, leave, eigen_x, eigen_yz, tables),
        1000 * cells,
    )
    modal = exchange(chunks, plan, plan.rows2)

    velocity_new, moments = call(
        functools.partial(project_kernel, plan),
        ((3,) + block, (3, plan.boxes)),
        (modal, star, stay, halves(backward), place),
        100 * cells,
    )
    return (velocity_new, theta_new, vapour_new, moments)


def solution(mesh):
    placed = (
        P(None, "gx", "gy", None),
        P("gx", "gy", None),
        P("gx", "gy", None),
        P(None, ("gx", "gy")),
        P(None, ("gx", "gy")),
        P(("gx", "gy")),
        P(("gx", "gy"), None),
        P(None, ("gx", "gy")),
    )
    return jax.shard_map(
        shards,
        mesh=mesh,
        in_specs=placed,
        out_specs=(
            P(None, "gx", "gy", None),
            P("gx", "gy", None),
            P("gx", "gy", None),
            P(None, ("gx", "gy")),
        ),
        check_vma=False,
    )
```

```python
import functools
import math

import jax
import jax.numpy as jnp
import ml_dtypes
import numpy as np
from jax import lax
from jax.experimental import pallas as pl
from jax.experimental.pallas import tpu as pltpu
from jax.sharding import PartitionSpec as P

BW = 4
LANES = 128

TIME_STEP = 0.2
DIFFUSION = 0.05
BUOYANCY = 0.5
GROWTH = 0.5
COLLISION = 0.05
CONDENSE = 0.002

VMEM = pl.BlockSpec(memory_space=pltpu.VMEM)
HBM = pl.BlockSpec(memory_space=pltpu.HBM)
NT = (((1,), (1,)), ((), ()))
TN = (((0,), (0,)), ((), ()))
NN = (((1,), (0,)), ((), ()))

KINDS = [(sx, sy) for sx in (-1, 0, 1) for sy in (-1, 0, 1) if (sx, sy) != (0, 0)]


def thirds(table):
    parts = []
    for _ in range(3):
        parts.append(table.astype(np.float32).astype(ml_dtypes.bfloat16))
        table = table - parts[-1].astype(np.float64)
    return np.concatenate(parts, axis=0)


def on_left(parts):
    return jnp.concatenate([parts] * 3, axis=1)


def on_right(parts):
    size = parts.shape[0] // 3
    once = jnp.concatenate([parts[i * size : (i + 1) * size] for i in range(3)], axis=1)
    return jnp.concatenate([once] * 3, axis=0)


def split(value, axis):
    parts = []
    for _ in range(3):
        parts.append(value.astype(jnp.bfloat16))
        value = value - parts[-1].astype(jnp.float32)
    return jnp.concatenate(parts, axis=axis)


def from_left(table, value, turned=False):
    out = lax.dot_general(
        table, split(value, 1 if turned else 0), NT if turned else NN,
        preferred_element_type=jnp.float32,
    )
    rows = out.shape[0] // 3
    return out[:rows] + (out[rows : 2 * rows] + out[2 * rows :])


def from_right(value, table, turned=False):
    out = lax.dot_general(
        split(value, 0 if turned else 1), table, TN if turned else NN,
        preferred_element_type=jnp.float32,
    )
    columns = out.shape[1] // 3
    return out[:, :columns] + (out[:, columns : 2 * columns] + out[:, 2 * columns :])


def real_basis(length):
    position = np.arange(length)[:, None]
    column = np.arange(length)
    wave = np.where(column <= length // 2, column, column - length // 2)
    angle = 2.0 * np.pi * ((position * wave[None, :]) % length) / length
    table = np.where(column[None, :] <= length // 2, np.cos(angle), np.sin(angle))
    table = table * np.sqrt(2.0 / length)
    table[:, 0] *= np.sqrt(0.5)
    if length % 2 == 0:
        table[:, length // 2] *= np.sqrt(0.5)
    return table, -4.0 * np.sin(np.pi * wave / length) ** 2


class Plan:
    def __init__(self, grid_x, grid_y, span_x, span_y, levels, slots):
        self.gx, self.gy = grid_x, grid_y
        self.sx, self.sy, self.nz = span_x, span_y, levels
        self.nd = grid_x * grid_y
        self.per = levels // self.nd
        self.x4 = LANES // span_y
        self.xg = span_x // self.x4
        self.main = self.per * self.xg
        self.rows1 = self.main + 1
        self.rows2 = self.main + 1
        self.tx, self.ty = grid_x * span_x, grid_y * span_y
        self.bx, self.by = span_x // BW, span_y // BW
        self.boxes = self.bx * self.by
        self.slots = slots
        self.width = 2 * self.by + 2 * self.bx + 4
        self.edge = 3 * self.width
        assert max(self.edge + 3 * self.per + 1, self.boxes + self.width) <= LANES

    def tables(self):
        nd, per, nz = self.nd, self.per, self.nz
        z = np.arange(nz)
        cosine = np.cos(np.pi / nz * (((2 * z[:, None] + 1) * z[None, :]) % (4 * nz)) / 2.0)
        mode = (np.arange(nd)[None, :] * per + np.arange(per)[:, None]).reshape(-1)
        forward = cosine.T[mode]
        weight = np.where(np.arange(nz) == 0, 1.0, 2.0) / nz
        backward = forward * weight[mode][:, None]
        qx, ex = real_basis(self.tx)
        qy, ey = real_basis(self.ty)
        q1 = qx.reshape(self.gx, self.xg, self.x4, self.tx)
        q1 = q1.transpose(3, 2, 1, 0).reshape(self.tx, self.tx)
        ez = -4.0 * np.sin(np.pi * z / (2 * nz)) ** 2
        return forward, backward, q1, qy, ex, ey, ez


def neighbours(count):
    first = [(i, i ^ 1) for i in range(count)]
    second = [(i, (i + 1) % count if i % 2 else (i - 1) % count) for i in range(count)]
    return first, second


def copy_all(copies):
    for copy in copies:
        copy.start()
    for copy in copies:
        copy.wait()


def planes_kernel(plan, vel, theta, vapour, xb, xa, sems):
    odd = lax.axis_index("gx") % 2
    copies = []
    for side, (out, x) in enumerate(((xb, odd), (xa, 1 - odd))):
        second = 1 + x * (plan.sx - 3)
        x = x * (plan.sx - 1)
        copies += [
            pltpu.make_async_copy(vel.at[0, second], out.at[5], sems.at[side, 3]),
            pltpu.make_async_copy(vel.at[:, x], out.at[0:3], sems.at[side, 0]),
            pltpu.make_async_copy(theta.at[x], out.at[3], sems.at[side, 1]),
            pltpu.make_async_copy(vapour.at[x], out.at[4], sems.at[side, 2]),
        ]
    for copy in copies:
        copy.start()
    for copy in copies:
        copy.wait()


def rows_kernel(plan, vel, theta, vapour, after, yb, ya):
    odd = lax.axis_index("gy") % 2 == 1
    for f, ref in enumerate((vel.at[0], vel.at[1], vel.at[2], theta, vapour)):
        for x in range(plan.sx):
            low, high = ref[x, 0:1], ref[x, plan.sy - 1 :]
            ya[f, x : x + 1] = jnp.where(odd, low, high)
            yb[f, x : x + 1] = jnp.where(odd, high, low)
    for x in range(plan.sx):
        low, high = vel[1, x, 1:2], vel[1, x, plan.sy - 2 : plan.sy - 1]
        ya[5, x : x + 1] = jnp.where(odd, low, high)
        yb[5, x : x + 1] = jnp.where(odd, high, low)


def edge_masks(plan):
    row = lax.broadcasted_iota(jnp.int32, (plan.sy, plan.nz), 0)
    lane = lax.broadcasted_iota(jnp.int32, (plan.sy, plan.nz), 1)
    return row == 0, row == plan.sy - 1, lane == 0, lane == plan.nz - 1


def coefficients(u, v, w):
    half = 0.5 * TIME_STEP
    side = TIME_STEP * DIFFUSION
    return (
        side - half * u, side + half * u,
        side - half * v, side + half * v,
        side - half * w, side + half * w,
    )


def advect(c, east, west, north_row, south_row, coef, masks, plan):
    row0, row_last, lane0, lane_last = masks
    north = jnp.where(row_last, north_row, pltpu.roll(c, plan.sy - 1, 0))
    south = jnp.where(row0, south_row, pltpu.roll(c, 1, 0))
    return weigh(c, east, west, north, south, coef, lane0, lane_last)


def weigh(c, east, west, north, south, coef, lane0, lane_last):
    upper = jnp.where(lane_last, c, pltpu.roll(c, c.shape[1] - 1, 1))
    lower = jnp.where(lane0, c, pltpu.roll(c, 1, 1))
    ce, cw, cn, cs, cu, cl = coef
    return (
        (1.0 - 6.0 * TIME_STEP * DIFFUSION) * c
        + (ce * east + cw * west)
        + (cn * north + cs * south)
        + (cu * upper + cl * lower)
    )


def side_planes(xa, xb, f):
    odd = lax.axis_index("gx") % 2 == 1
    return jnp.where(odd, xa[f], xb[f]), jnp.where(odd, xb[f], xa[f])


def side_rows(ya, yb, f):
    odd = lax.axis_index("gy") % 2 == 1
    return jnp.where(odd, ya[f], yb[f]), jnp.where(odd, yb[f], ya[f])


def before(value, axis):
    at = lax.broadcasted_iota(jnp.int32, value.shape, axis)
    return jnp.where(at == 0, 0.0, pltpu.roll(value, 1, axis))


def inner_kernel(plan, vel, theta, div, along_x, along_y):
    masks = edge_masks(plan)
    zero = jnp.zeros((plan.sy, plan.nz), jnp.float32)
    zero_row = jnp.zeros((1, plan.nz), jnp.float32)
    last = plan.sx - 1
    last_u = None
    for x in range(plan.sx):
        coef = coefficients(vel[0, x], vel[1, x], vel[2, x])
        u, v, w = (
            advect(
                vel[f, x],
                vel[f, x + 1] if x < last else zero,
                vel[f, x - 1] if x else zero,
                zero_row, zero_row, coef, masks, plan,
            )
            for f in range(3)
        )
        w = w + (TIME_STEP * BUOYANCY) * theta[x]
        total = (u if last_u is None else u - last_u) + (v - before(v, 0)) + (w - before(w, 1))
        div[x] = total
        last_u = u
        along_y[0, x : x + 1] = v[plan.sy - 1 : plan.sy]
        along_y[1, x : x + 1] = coef[3][0:1]
        along_y[2, x : x + 1] = coef[2][plan.sy - 1 : plan.sy]
        along_y[3, x : x + 1] = vel[1, x, 0:1]
        if x == 0:
            along_x[1] = coef[1]
            along_x[3] = vel[0, x]
        if x == last:
            along_x[0] = u
            along_x[2] = coef[0]


def spread_kernel(plan, div, along_x, along_y, xb, yb, xa, ya, forward, out):
    sides = [side_planes(xa, xb, f) for f in range(3)]
    ends = [side_rows(ya, yb, f) for f in range(3)]
    west_u, west_v, west_w = (along_x[1] * west for west, _ in sides)
    east_u, east_v, east_w = (along_x[2] * east for _, east in sides)
    south_u, south_v, south_w = (along_y[1] * south for south, _ in ends)
    north_u, north_v, north_w = (along_y[2] * north for _, north in ends)
    first_row = south_u - before(south_u, 0) + south_v + south_w - before(south_w, 1)
    last_row = north_u - before(north_u, 0) + north_v + north_w - before(north_w, 1)
    row = lax.broadcasted_iota(jnp.int32, (plan.sy, plan.nz), 0)
    column = lax.broadcasted_iota(jnp.int32, (plan.sx, plan.nz), 0)
    level = lax.broadcasted_iota(jnp.int32, (plan.sx, plan.nz), 1)
    last = plan.sx - 1
    west = [side[0] for side in sides]
    none = jnp.zeros((1, plan.nz), jnp.float32)
    west_star = advect(
        west[0], along_x[3], side_planes(xa, xb, 5)[0], none, none, coefficients(*west),
        edge_masks(plan), plan,
    )
    south = [end[0] for end in ends]
    south_star = weigh(
        south[1],
        jnp.where(column == last, 0.0, pltpu.roll(south[1], plan.sx - 1, 0)),
        before(south[1], 0),
        along_y[3],
        side_rows(ya, yb, 5)[0],
        coefficients(*south),
        level == 0,
        level == plan.nz - 1,
    )
    first_row = first_row - south_star
    slab = []
    for x in range(plan.sx):
        at = slice(x, x + 1)
        total = div[x] + jnp.where(
            row == 0,
            first_row[at],
            jnp.where(
                row == 1, -south_v[at], jnp.where(row == plan.sy - 1, last_row[at], 0.0)
            ),
        )
        if x == 0:
            total = total - west_star + west_u + (west_v - before(west_v, 0)) + (west_w - before(west_w, 1))
        if x == 1:
            total = total - west_u
        if x == last:
            total = total + east_u + (east_v - before(east_v, 0)) + (east_w - before(east_w, 1))
        slab.append(total)
    corners = (
        south_u[last:], north_u[last:], west_v[plan.sy - 1 :], east_v[plan.sy - 1 :]
    )
    block = jnp.zeros((plan.sy, plan.nz), jnp.float32)
    for k, corner in enumerate(corners):
        block = jnp.where(row == k, -corner, block)
    modes = from_left(
        on_left(forward[...]), jnp.concatenate(slab + [block] * plan.x4, axis=0), turned=True
    )
    for g in range(plan.xg):
        for j in range(plan.per):
            out[pl.ds(j * plan.xg + g, plan.nd, stride=plan.rows1), :] = modes[
                j * plan.nd : (j + 1) * plan.nd, g * LANES : (g + 1) * LANES
            ]
    extra = modes[:, plan.xg * LANES :]
    lane = lax.broadcasted_iota(jnp.int32, (plan.nd, LANES), 1)
    total = jnp.zeros((plan.nd, LANES), jnp.float32)
    for j in range(plan.per):
        part = extra[j * plan.nd : (j + 1) * plan.nd]
        total = jnp.where(lane // plan.sy == j, part, total)
    out[pl.ds(plan.main, plan.nd, stride=plan.rows1), :] = total


def regroup(parts, plan):
    group = lax.broadcasted_iota(jnp.int32, parts[0].shape, 1) // plan.sy
    parts = list(parts)
    distance = plan.x4 // 2
    while distance:
        lower = group & distance == 0
        step = distance * plan.sy
        for i in range(plan.x4):
            if not i & distance:
                one, two = parts[i], parts[i + distance]
                parts[i] = jnp.where(lower, one, pltpu.roll(two, step, 1))
                parts[i + distance] = jnp.where(lower, pltpu.roll(one, LANES - step, 1), two)
        distance //= 2
    return parts


def solve_kernel(plan, r, leave, eigen_x, eigen_yz, tables, out):
    wide_x, wide_y = 3 * plan.tx, 3 * plan.ty
    fy, by = (on_right(tables[i, :wide_y, : plan.ty]) for i in (0, 1))
    fx, bx = (on_left(tables[i, :wide_x, : plan.tx]) for i in (2, 3))
    rank = lax.axis_index("gx") * plan.gy + lax.axis_index("gy")
    eigen = eigen_x[...] + eigen_yz[pl.ds(rank, 1), :]
    inverse = jnp.where(eigen == 0.0, 0.0, 1.0 / jnp.where(eigen == 0.0, 1.0, eigen))
    gx, gy, per, xg, x4 = plan.gx, plan.gy, plan.per, plan.xg, plan.x4
    lane = lax.broadcasted_iota(jnp.int32, (gx, LANES), 1)
    step1, step2 = gy * plan.rows1, gy * plan.rows2

    def take(b, q):
        return r[pl.ds(b * plan.rows1 + q, gx, stride=step1), :]

    def moved(block, source, target):
        return pltpu.roll(jnp.where(lane == source, block, 0.0), (target - source) % LANES, 1)

    blocks = [[take(b, q) for q in range(plan.main)] for b in range(gy)]
    for b in range(gy):
        here = take(b, plan.main)
        ahead = pltpu.roll(here, 1, 0)
        nb = (b + 1) % gy
        for j in range(per):
            at, first, final = j * plan.sy, j * xg, j * xg + xg - 1
            blocks[b][first] = blocks[b][first] + (
                moved(ahead, at, 0) + moved(ahead, at + 1, plan.sy - 1)
            )
            blocks[nb][first] = blocks[nb][first] + moved(here, at + 2, 0)
            blocks[nb][final] = blocks[nb][final] + moved(here, at + 3, (x4 - 1) * plan.sy)
    turned = [
        [regroup([blocks[h + i][q] for i in range(x4)], plan) for h in range(0, gy, x4)]
        for q in range(plan.main)
    ]
    grid = jnp.concatenate(
        [
            jnp.concatenate([part[p] for part in turned[q]], axis=1)
            for p in range(x4)
            for q in range(plan.main)
        ],
        axis=0,
    )
    in_y = from_right(grid, fy)
    height = xg * gx

    def piece(value, row, column):
        return value[row * height : (row + 1) * height, column * plan.ty : (column + 1) * plan.ty]

    in_y = jnp.concatenate(
        [
            jnp.concatenate([piece(in_y, p * per + j, 0) for p in range(x4)], axis=0)
            for j in range(per)
        ],
        axis=1,
    )
    spectrum = from_left(fx, in_y)
    solved = spectrum * inverse
    in_x = from_left(bx, solved)
    in_x = jnp.concatenate([piece(in_x, p, j) for p in range(x4) for j in range(per)], axis=0)
    grid = from_right(in_x, by)
    blocks = [[None] * plan.main for _ in range(gy)]
    for q in range(plan.main):
        for h in range(0, gy, x4):
            parts = [
                grid[
                    (p * plan.main + q) * gx : (p * plan.main + q + 1) * gx,
                    h * plan.sy : h * plan.sy + LANES,
                ]
                for p in range(x4)
            ]
            for i, part in enumerate(regroup(parts, plan)):
                blocks[h + i][q] = part
    scale = 1.0 / (plan.nz * math.sqrt(plan.tx * plan.ty))
    mean = jnp.where(rank == 0, spectrum[0:1, 0:1] * scale, 0.0)
    mean = jnp.where(lane == plan.edge + 3 * per, mean, 0.0)

    for b in range(gy):
        for q in range(plan.main):
            out[pl.ds(b * plan.rows2 + q, gx, stride=step2), :] = blocks[b][q]
        along_x = jnp.zeros((gx, LANES), jnp.float32)
        row = leave[pl.ds(b, gx, stride=gy), :] + mean
        for j in range(per):
            here = blocks[b][j * xg]
            along_x = along_x + moved(here, 0, plan.edge + j)
            along_x = along_x + moved(here, plan.sy - 1, plan.edge + 2 * per + j)
            row = row + moved(blocks[(b + 1) % gy][j * xg], 0, plan.edge + per + j)
        out[pl.ds(b * plan.rows2 + plan.main, gx, stride=step2), :] = row + pltpu.roll(
            along_x, gx - 1, 0
        )


def project_kernel(plan, r, star, stay, backward, place, vel_new, moments):
    nd, per, xg, sy, sx = plan.nd, plan.per, plan.xg, plan.sy, plan.sx
    lane = lax.broadcasted_iota(jnp.int32, (nd, LANES), 1) - plan.edge

    def take(q):
        return r[pl.ds(q, nd, stride=plan.rows2), :]

    row = take(plan.main)
    beyond = (lane >= 0) & (lane < 3 * per)
    beyond = [jnp.where(beyond & (lane % per == j), row, 0.0) for j in range(per)]
    modes = [
        jnp.concatenate([take(j * xg + g) for j in range(per)], axis=0) for g in range(xg)
    ]
    modes.append(jnp.concatenate(beyond, axis=0))
    cells = from_right(jnp.concatenate(modes, axis=1), on_right(backward[...]), turned=True)

    def cell(k):
        at = xg * LANES + plan.edge + k * per
        return functools.reduce(jnp.add, [cells[at + j : at + j + 1] for j in range(per)])

    east_first, north_first, east_last = cell(0), cell(1), cell(2)
    came = jnp.sum(row, axis=0, keepdims=True)
    mean = came[:, plan.edge + 3 * per : plan.edge + 3 * per + 1]
    pressure = [cells[x * sy : (x + 1) * sy] for x in range(sx)]
    y = lax.broadcasted_iota(jnp.int32, (sy, plan.nz), 0)
    z = lax.broadcasted_iota(jnp.int32, (sy, plan.nz), 1)
    ends = slice(sy - 8, sy)
    u_before = None
    for x in range(sx):
        here = pressure[x]
        upper = jnp.where(z == plan.nz - 1, here, pltpu.roll(here, plan.nz - 1, 1))
        w = star[2, x] - (upper - here)
        along_z = w - before(w, 1)
        v = star[1, x] - (pltpu.roll(here, sy - 1, 0) - here)
        if x < sx - 1:
            u = star[0, x] - (pressure[x + 1] - here)
        else:
            u = u_before - (v - pltpu.roll(v, 1, 0)) - along_z + mean
            u = jnp.where(y == 0, star[0, x] - (east_first - here), u)
            u = jnp.where(y == sy - 1, star[0, x] - (east_last - here), u)
        if x == 0:
            v_last = star[1, x, ends] - (north_first - here[ends])
        else:
            v_last = pltpu.roll(v[ends], 1, 0) - (u[ends] - u_before[ends]) - along_z[ends] + mean
        v_last = jnp.where(y[ends] == sy - 1, v_last, v[ends])
        vel_new[0, x] = u
        vel_new[1, x, : sy - 8] = v[: sy - 8]
        vel_new[1, x, sy - 8 :] = v_last
        vel_new[2, x] = w
        u_before = u
    load = lax.broadcasted_iota(jnp.int32, (8, LANES), 0)
    at = lax.broadcasted_iota(jnp.int32, (8, LANES), 1)
    loads = jnp.where(at // plan.width == load, came, 0.0)
    total = stay[...] + lax.dot_general(
        loads, place[...], NN, precision=lax.Precision.HIGHEST, preferred_element_type=jnp.float32
    )
    moments[...] = total[:3, : plan.boxes] * (1.0 / plan.slots)


def droplet_tables(plan):
    bx, by, boxes = plan.bx, plan.by, plan.boxes
    width = plan.width
    lane_of = {}
    kind_of = np.full((LANES,), -1)
    place = np.zeros((LANES, LANES), np.float32)
    for k, (sx, sy) in enumerate(KINDS):
        xs = range(bx) if sx == 0 else [0 if sx > 0 else bx - 1]
        ys = range(by) if sy == 0 else [0 if sy > 0 else by - 1]
        for x in xs:
            for y in ys:
                lane_of[k, x, y] = len(lane_of)
    assert len(lane_of) == width
    for (k, x, y), at in lane_of.items():
        for load in range(3):
            kind_of[load * width + at] = k
            place[load * width + at, x * by + y] = 1.0
    goes = np.zeros((9 * boxes, LANES), np.float32)
    for dx in (-1, 0, 1):
        for dy in (-1, 0, 1):
            code = (dx + 1) * 3 + dy + 1
            for x in range(bx):
                for y in range(by):
                    line = code * boxes + x * by + y
                    sx = (x + dx) // bx
                    sy = (y + dy) // by
                    tx, ty = (x + dx) % bx, (y + dy) % by
                    if (sx, sy) == (0, 0):
                        goes[line, tx * by + ty] = 1.0
                    else:
                        goes[line, boxes + lane_of[KINDS.index((sx, sy)), tx, ty]] = 1.0
    return goes, place, kind_of[None].astype(np.int32)


def quotient(value, divisor):
    if divisor & (divisor - 1) == 0:
        return value >> (divisor.bit_length() - 1), value & (divisor - 1)
    return lax.div(value, divisor), lax.rem(value, divisor)


def scalar_kernel(
    plan, vel, theta, vapour, xb, yb, xa, ya, radius, multiplicity, counts, pairing,
    destination, goes, kind, star, theta_new, vapour_new, stay, leave, moist,
):
    masks = edge_masks(plan)
    bx, by, boxes = plan.bx, plan.by, plan.boxes
    edges = []
    for f in range(5):
        west, east = side_planes(xa, xb, f)
        south, north = side_rows(ya, yb, f)
        edges.append((west, east, south, north))
    sums = []
    total = None
    for x in range(plan.sx):
        coef = coefficients(vel[0, x], vel[1, x], vel[2, x])
        for f, (west, east, south, north) in enumerate(edges):
            ref = (vel.at[0], vel.at[1], vel.at[2], theta, vapour)[f]
            new = (star.at[0], star.at[1], star.at[2], theta_new, moist)[f]
            moved = advect(
                ref[x],
                ref[x + 1] if x < plan.sx - 1 else east,
                ref[x - 1] if x else west,
                north[x : x + 1], south[x : x + 1], coef, masks, plan,
            )
            if f == 2:
                moved = moved + (TIME_STEP * BUOYANCY) * theta[x]
            new[x] = moved
        total = moved if x % BW == 0 else total + moved
        if x % BW == BW - 1:
            sums.append(jnp.sum(total, axis=1, keepdims=True))
    exact = functools.partial(
        lax.dot_general, dimension_numbers=NN, precision=lax.Precision.HIGHEST,
        preferred_element_type=jnp.float32,
    )
    gather_y = (
        lax.broadcasted_iota(jnp.int32, (by, plan.sy), 1) // BW
        == lax.broadcasted_iota(jnp.int32, (by, plan.sy), 0)
    ).astype(jnp.float32)
    spread_y = (
        lax.broadcasted_iota(jnp.int32, (plan.sy, by), 0) // BW
        == lax.broadcasted_iota(jnp.int32, (plan.sy, by), 1)
    ).astype(jnp.float32)
    means = jnp.concatenate(
        [exact(gather_y, jnp.broadcast_to(s, (plan.sy, LANES))) for s in sums], axis=0
    ) * (1.0 / (BW * BW * plan.nz))
    softplus = jnp.maximum(means, 0.0) + jnp.log(1.0 + jnp.exp(-jnp.abs(means)))
    rank_x, rank_y = lax.axis_index("gx"), lax.axis_index("gy")
    box = lax.broadcasted_iota(jnp.int32, (boxes, plan.slots), 0)
    slot = lax.broadcasted_iota(jnp.int32, (boxes, plan.slots), 1)
    device, local = quotient(destination[...], boxes)
    device_x, device_y = quotient(device, plan.gy)
    local_x, local_y = quotient(local, by)
    source_x, source_y = quotient(box, by)
    offset_x = (device_x - rank_x) * bx + local_x - source_x + (1 + bx * plan.gx)
    offset_y = (device_y - rank_y) * by + local_y - source_y + (1 + by * plan.gy)
    offset_x = quotient(offset_x, bx * plan.gx)[1]
    offset_y = quotient(offset_y, by * plan.gy)[1]
    code = (offset_x * 3 + offset_y).astype(jnp.float32)
    line = lax.broadcasted_iota(jnp.int32, (boxes, boxes), 0)
    used = jnp.where(
        line == lax.broadcasted_iota(jnp.int32, (boxes, boxes), 1), counts[...], 0
    )
    used = jnp.sum(used, axis=1, keepdims=True)
    live = jnp.where(slot < used, multiplicity[...], 0.0)
    half = plan.slots // 2
    order = pairing[...]
    index = jnp.concatenate([order, order[:, half:], order[:, :half]], axis=1)

    def gather(value):
        twice = jnp.concatenate([value, value], axis=1)
        return jnp.take_along_axis(twice, index, axis=1, mode="promise_in_bounds")

    radius_sq, live, code = gather(radius[...]), gather(live), gather(code)
    grown_sq = radius_sq + GROWTH * softplus
    root = jnp.sqrt(grown_sq)
    mass = grown_sq * root
    lane = lax.broadcasted_iota(jnp.int32, (boxes, LANES), 1)
    own = lane < plan.slots
    condensed = jnp.sum(
        jnp.where(own, live * (mass - radius_sq * jnp.sqrt(radius_sq)), 0.0),
        axis=1, keepdims=True,
    )
    condensed = jnp.broadcast_to(condensed, (boxes, LANES))
    for big in range(bx):
        less = CONDENSE * exact(spread_y, condensed[big * by : (big + 1) * by])
        for x in range(big * BW, (big + 1) * BW):
            vapour_new[x] = moist[x] - less

    def partner(value):
        return pltpu.roll(value, LANES - plan.slots, 1)

    other_grown, other_root, other_mass = partner(grown_sq), partner(root), partner(mass)
    both = root + other_root
    rate = both * both * jnp.abs(grown_sq - other_grown) * partner(live)
    final = (mass + COLLISION * rate * other_mass) / (1.0 + COLLISION * rate)
    weight = jnp.where(own, live, 0.0)
    loads = (weight, weight * final, weight * final * final)
    parts = [[], [], []]
    for direction in range(9):
        chosen = code == float(direction)
        for k in range(3):
            parts[k].append(
                jnp.sum(jnp.where(chosen, loads[k], 0.0), axis=1, keepdims=True)
            )
    payload = jnp.zeros((1, LANES), jnp.float32)
    stays = jnp.zeros((8, LANES), jnp.float32)
    line = lax.broadcasted_iota(jnp.int32, (8, LANES), 0)
    lane = lax.broadcasted_iota(jnp.int32, (1, LANES), 1)
    width = plan.width
    leaving = (lane >= boxes) & (lane < boxes + width)
    for k in range(3):
        column = jnp.concatenate(parts[k], axis=0)
        landed = jnp.sum(column * goes[...], axis=0, keepdims=True)
        stays = jnp.where(line == k, landed, stays)
        payload = payload + pltpu.roll(
            jnp.where(leaving, landed, 0.0), (k * width - boxes) % LANES, 1
        )
    stay[...] = stays
    owner = jnp.full((1, LANES), -1, jnp.int32)
    for k, (sx, sy) in enumerate(KINDS):
        to_x = lax.rem(rank_x + (sx + plan.gx), plan.gx)
        to_y = lax.rem(rank_y + (sy + plan.gy), plan.gy)
        owner = jnp.where(kind[...] == k, to_x * plan.gy + to_y, owner)
    every = lax.broadcasted_iota(jnp.int32, (plan.nd, LANES), 0)
    leave[...] = jnp.where(every == owner, payload, 0.0)


def call(body, outs, args, flops, scratch=(), space=VMEM):
    moved = sum(a.size * a.dtype.itemsize for a in args)
    moved += sum(math.prod(o) * 4 for o in outs)
    return pl.pallas_call(
        body,
        out_shape=[jax.ShapeDtypeStruct(o, jnp.float32) for o in outs],
        in_specs=[space] * len(args),
        out_specs=[VMEM] * len(outs),
        scratch_shapes=list(scratch),
        compiler_params=pltpu.CompilerParams(vmem_limit_bytes=16 * 2**20),
        cost_estimate=pl.CostEstimate(flops=flops, bytes_accessed=moved, transcendentals=0),
    )(*args)


def exchange(chunks, plan, rows):
    flat = chunks.reshape(plan.nd, 1, rows * LANES)
    flat = lax.all_to_all(flat, ("gx", "gy"), split_axis=0, concat_axis=0, tiled=True)
    return flat.reshape(plan.nd * rows, LANES)


def shards(velocity, theta, vapour, radius_sq, multiplicity, counts, pairing, destination):
    span_x, span_y, levels = theta.shape
    slots = radius_sq.shape[0]
    plan = Plan(lax.axis_size("gx"), lax.axis_size("gy"), span_x, span_y, levels, slots)
    forward, backward, q1, qy, ex, ey, ez = plan.tables()
    goes, place, kind = droplet_tables(plan)
    block = (span_x, span_y, levels)
    cells = math.prod(block)

    plane, rows = (6, span_y, levels), (6, span_x, levels)
    fields = (velocity, theta, vapour)
    placed = [pltpu.with_memory_space_constraint(f, pltpu.HBM) for f in fields]
    xb, xa = call(
        functools.partial(planes_kernel, plan), (plane, plane), placed, cells,
        [pltpu.SemaphoreType.DMA((2, 4))], HBM,
    )
    yb, ya = call(functools.partial(rows_kernel, plan), (rows, rows), (*fields, xa), cells)
    ways_x, ways_y = neighbours(plan.gx), neighbours(plan.gy)
    xb, xa = lax.ppermute(xb, "gx", ways_x[1]), lax.ppermute(xa, "gx", ways_x[0])
    yb, ya = lax.ppermute(yb, "gy", ways_y[1]), lax.ppermute(ya, "gy", ways_y[0])
    halo = (xb, yb, xa, ya)

    inner = call(
        functools.partial(inner_kernel, plan),
        (block, (4, span_y, levels), (4, span_x, levels)), (velocity, theta), 100 * cells,
    )
    (chunks,) = call(
        functools.partial(spread_kernel, plan), ((plan.nd * plan.rows1, LANES),),
        (*inner, *halo, thirds(forward)), 100 * cells,
    )
    spectral = exchange(chunks, plan, plan.rows1)

    tables = [thirds(qy), thirds(qy.T), thirds(q1), thirds(q1.T)]
    rows, columns = (max(t.shape[i] for t in tables) for i in (0, 1))
    tables = np.stack(
        [np.pad(t, ((0, rows - t.shape[0]), (0, columns - t.shape[1]))) for t in tables]
    )
    eigen_x = ex.astype(np.float32)[:, None]
    eigen_yz = (ez.reshape(plan.nd, plan.per, 1) + ey).reshape(plan.nd, -1).astype(np.float32)
    star, theta_new, vapour_new, stay, leave = call(
        functools.partial(scalar_kernel, plan),
        ((3,) + block, block, block, (8, LANES), (plan.nd, LANES)),
        fields + halo + (radius_sq.T, multiplicity.T, counts[None], pairing)
        + (destination.T, goes, kind),
        100 * cells,
        (pltpu.VMEM(block, jnp.float32),),
    )

    (chunks,) = call(
        functools.partial(solve_kernel, plan),
        ((plan.nd * plan.rows2, LANES),),
        (spectral, leave, eigen_x, eigen_yz, tables),
        1000 * cells,
    )
    modal = exchange(chunks, plan, plan.rows2)

    velocity_new, moments = call(
        functools.partial(project_kernel, plan),
        ((3,) + block, (3, plan.boxes)),
        (modal, star, stay, thirds(backward), place),
        100 * cells,
    )
    return (velocity_new, theta_new, vapour_new, moments)


def solution(mesh):
    placed = (
        P(None, "gx", "gy", None),
        P("gx", "gy", None),
        P("gx", "gy", None),
        P(None, ("gx", "gy")),
        P(None, ("gx", "gy")),
        P(("gx", "gy")),
        P(("gx", "gy"), None),
        P(None, ("gx", "gy")),
    )
    return jax.shard_map(
        shards,
        mesh=mesh,
        in_specs=placed,
        out_specs=(
            P(None, "gx", "gy", None),
            P("gx", "gy", None),
            P("gx", "gy", None),
            P(None, ("gx", "gy")),
        ),
        check_vma=False,
    )
```
